128 devices in a mesh: seq: 32 (over y, x, core), opt: 4 (over z).
Axes of the slice: x: 4, y: 4, z: 4, core: 2. Of those that a mesh axis runs over, the one named last changes fastest.
Arguments:
- image: float32 [8, 4096, 256], P('opt', 'seq'), may hold values from -6 to 6
- labels: int32 [8, 7], P('opt'), may hold values from 0 to 3
- coords: int32 [8, 7, 2], P('opt'), may hold values from 0 to 1023
- fourier: float32 [2, 128], replicated, may hold values from -5 to 5
- self_weights: float32 [4, 256, 256], replicated, may hold values from -0.5 to 0.5
- cross_weights: float32 [8, 256, 128], replicated
- mlp_weights: float32 [2, 2048, 256], replicated
- vectors: float32 [5376], replicated
- query_cot: float32 [8, 7, 256], P('opt'), may hold values from -6 to 6
- key_cot: float32 [8, 4096, 256], P('opt', 'seq'), may hold values from -6 to 6
- self_moment: float32 [4, 256, 256], P(None, 'opt')
- cross_moment: float32 [8, 256, 128], P(None, 'opt')
- mlp_moment: float32 [2, 2048, 256], P(None, 'opt')
- vec_first: float32 [5376], P('opt')
- vec_second: float32 [5376], P('opt')
Outputs:
- queries_out: float32 [8, 7, 256], P('opt')
- keys_out: float32 [8, 4096, 256], P('opt', 'seq')
- image_grad: float32 [8, 4096, 256], P('opt', 'seq')
- self_moment_new: float32 [4, 256, 256], P(None, 'opt')
- self_new: float32 [4, 256, 256], P(None, 'opt')
- cross_moment_new: float32 [8, 256, 128], P(None, 'opt')
- cross_new: float32 [8, 256, 128], P(None, 'opt')
- mlp_moment_new: float32 [2, 2048, 256], P(None, 'opt')
- mlp_new: float32 [2, 2048, 256], P(None, 'opt')
- vec_first_new: float32 [5376], P('opt')
- vec_second_new: float32 [5376], P('opt')
- vectors_new: float32 [5376], P('opt')
The draws below stay inside these ranges and needn't reach their ends.
All inputs are finite; a program needn't handle non-finite values.
Results may differ from the reference program's by a relative error of at most 0.0003.
Values sent between devices are 32-bit elements; how exact they have to be, the bound alone decides.
A program may use at most 128 MiB of HBM per device.

```python
import math
import jax
import jax.numpy as jnp
from jax import lax

D = 256
HEADS = 8
CROSS = 128
FF = 2048
P_SIZE = 7
IMG = 1024
NS_ITERS = 5
STEP = 10
LEN = 4096
SLICES = 8
VEC = 5376


def gradient_sizes():
    prompt_rows = math.sqrt(SLICES * P_SIZE)
    image_rows = math.sqrt(SLICES * LEN)
    return (prompt_rows, image_rows)


def cross_scales():
    prompt_rows, image_rows = gradient_sizes()
    thin_side = prompt_rows / math.sqrt(LEN)
    return jnp.array([0.3 * prompt_rows, thin_side, thin_side, 0.1 * prompt_rows, 0.1 * image_rows, 0.1 * image_rows, 0.1 * image_rows, 0.3 * image_rows], jnp.float32)


def vector_scales():
    prompt_rows, image_rows = gradient_sizes()
    norm_part = jnp.concatenate([jnp.full((3 * D,), 0.5 * prompt_rows, jnp.float32), jnp.full((D,), 0.3 * image_rows, jnp.float32)])
    return jnp.concatenate([norm_part, norm_part, jnp.full((FF,), 0.3 * prompt_rows, jnp.float32), jnp.full((D,), 0.5 * prompt_rows, jnp.float32), jnp.full((4 * D,), 0.5 * prompt_rows, jnp.float32)])


def draw_cross_weights(key, part):
    key = jax.random.fold_in(key, 11)
    narrow = (D / 2.0) ** (-0.5)
    member = jnp.array([narrow, narrow, narrow, math.sqrt(LEN) / (8.0 * math.sqrt(CROSS)), narrow, narrow, narrow, 1.5 / math.sqrt(CROSS)], jnp.float32)
    return jax.random.normal(key, (8, D, CROSS), jnp.float32) * member[:, None, None]


def draw_mlp_weights(key, part):
    key = jax.random.fold_in(key, 12)
    member = jnp.array([1.5 / math.sqrt(D), 1.2 / math.sqrt(FF)], jnp.float32)
    return jax.random.normal(key, (2, FF, D), jnp.float32) * member[:, None, None]


def draw_vectors(key, part):
    key = jax.random.fold_in(key, 13)
    subkeys = jax.random.split(key, 5)
    norm_gains = jax.random.uniform(subkeys[0], (4 * D,), jnp.float32, 0.6, 1.4)
    biases = 0.3 * jax.random.normal(subkeys[1], (4 * D,), jnp.float32)
    bias_up = 0.3 * jax.random.normal(subkeys[2], (FF,), jnp.float32)
    bias_down = 0.3 * jax.random.normal(subkeys[3], (D,), jnp.float32)
    label_rows = jax.random.normal(subkeys[4], (4 * D,), jnp.float32)
    return jnp.concatenate([norm_gains, biases, bias_up, bias_down, label_rows])


def draw_self_moment(key, part):
    key = jax.random.fold_in(key, 14)
    prompt_rows, image_rows = gradient_sizes()
    return 0.3 * prompt_rows * jax.random.normal(key, (4, D, D), jnp.float32)


def draw_cross_moment(key, part):
    key = jax.random.fold_in(key, 15)
    return jax.random.normal(key, (8, D, CROSS), jnp.float32) * cross_scales()[:, None, None]


def draw_mlp_moment(key, part):
    key = jax.random.fold_in(key, 16)
    prompt_rows, image_rows = gradient_sizes()
    return 0.3 * prompt_rows * jax.random.normal(key, (2, FF, D), jnp.float32)


def draw_vec_first(key, part):
    key = jax.random.fold_in(key, 17)
    return 0.1 / 0.9 * vector_scales() * jax.random.normal(key, (VEC,), jnp.float32)


def draw_vec_second(key, part):
    key = jax.random.fold_in(key, 18)
    scales = vector_scales()
    return 0.001 / 0.999 * scales * scales * jax.random.uniform(key, (VEC,), jnp.float32, 1.0, 4.0)


def touch_ends(entries, stream_key, smallest, top_value):
    shape = entries.shape
    spot = [jax.random.randint(jax.random.fold_in(stream_key, axis), (), 0, shape[axis]) for axis in range(len(shape))]
    entries = entries.at[tuple(spot)].set(smallest)
    longest = shape.index(max(shape))
    spot[longest] = (spot[longest] + 1) % shape[longest]
    return entries.at[tuple(spot)].set(top_value)


def block_scale(own_key, dims, shards, low, largest):
    def one(axis_at, blocks):
        draws = jax.random.uniform(jax.random.fold_in(jax.random.fold_in(own_key, 6), axis_at), (blocks,), jnp.float32, low / len(shards), largest / len(shards))
        return jnp.repeat(jnp.exp(draws), dims[axis_at] // blocks).reshape((-1,) + (1,) * (len(dims) - axis_at - 1))

    factor_of = one(*shards[0])
    for cut in shards[1:]:
        factor_of = factor_of * one(*cut)
    return factor_of


def scatter_about(rng, extent, width, most, cuts=(), kind=jnp.bfloat16):
    result = jax.random.normal(rng, extent, jnp.float32) * width
    if len(cuts) > 0:
        result = block_scale(rng, extent, cuts, -0.22, 0.18) * result
    return jnp.clip(result, min=-most, max=most).astype(kind)


def setup_inputs(seed: int = 0) -> dict:
    keys = jax.random.split(jax.random.key(seed), 16)
    return {
        "image": scatter_about(keys[0], (SLICES, LEN, D), 1.0, 6.0, ((0, 4), (1, 32)), jnp.float32),
        "labels": touch_ends(jax.random.randint(keys[1], (SLICES, P_SIZE), 0, 4), jax.random.fold_in(keys[1], 1), 0, 3).astype(jnp.int32),
        "coords": touch_ends(jax.random.randint(keys[2], (SLICES, P_SIZE, 2), 0, IMG), jax.random.fold_in(keys[2], 1), 0, IMG - 1).astype(jnp.int32),
        "fourier": scatter_about(keys[3], (2, D // 2), 1.0, 5.0, (), jnp.float32),
        "self_weights": scatter_about(keys[4], (4, D, D), (D // 2) ** -0.5, 0.5, (), jnp.float32),
        "cross_weights": draw_cross_weights(jax.random.fold_in(keys[15], 71), 0),
        "mlp_weights": draw_mlp_weights(jax.random.fold_in(keys[15], 71), 0),
        "vectors": draw_vectors(jax.random.fold_in(keys[15], 71), 0),
        "query_cot": scatter_about(keys[8], (SLICES, P_SIZE, D), 1.0, 6.0, ((0, 4),), jnp.float32),
        "key_cot": scatter_about(keys[9], (SLICES, LEN, D), 1.0, 6.0, ((0, 4), (1, 32)), jnp.float32),
        "self_moment": draw_self_moment(jax.random.fold_in(keys[15], 71), 0),
        "cross_moment": draw_cross_moment(jax.random.fold_in(keys[15], 71), 0),
        "mlp_moment": draw_mlp_moment(jax.random.fold_in(keys[15], 71), 0),
        "vec_first": draw_vec_first(jax.random.fold_in(keys[15], 71), 0),
        "vec_second": draw_vec_second(jax.random.fold_in(keys[15], 71), 0),
    }


HIGHEST = lax.Precision.HIGHEST
NORM_EPSILON = 1e-05
COEF_LINEAR = 3.4445
COEF_CUBIC = -4.775
COEF_QUINTIC = 2.0315
MOMENTUM_DECAY = 0.95
MATRIX_RATE = 0.05
MATRIX_DECAY = 0.01
SCALE_EPSILON = 1e-07
VECTOR_RATE = 0.1
FIRST_DECAY = 0.9
SECOND_DECAY = 0.999
VECTOR_EPSILON = 1e-08

def matmul(left, right):
    return jnp.dot(left, right, precision=HIGHEST)

def layer_norm(inputs, gain, bias):
    center = inputs - lax.optimization_barrier(jnp.mean(inputs, axis=-1, keepdims=True))
    spread = lax.optimization_barrier(jnp.mean(center * center, axis=-1, keepdims=True))
    return center * lax.rsqrt(spread + NORM_EPSILON) * gain + bias

def to_heads(inputs):
    return inputs.reshape(inputs.shape[0], HEADS, inputs.shape[1] // HEADS).transpose(1, 0, 2)

def from_heads(inputs):
    return inputs.transpose(1, 0, 2).reshape(inputs.shape[1], inputs.shape[0] * inputs.shape[2])

def attention(queries, key_heads, values):
    factor = 1.0 / math.sqrt(queries.shape[-1])
    scores = jnp.einsum('hqd,hkd->hqk', queries, key_heads, precision=HIGHEST) * factor
    shifted = jnp.exp(scores - lax.optimization_barrier(jnp.max(scores, axis=-1, keepdims=True)))
    weights = shifted / lax.optimization_barrier(jnp.sum(shifted, axis=-1, keepdims=True))
    return jnp.einsum('hqk,hkd->hqd', weights, values, precision=HIGHEST)

def unpack(vector_set):
    norm_gains = vector_set[:4 * D].reshape(4, D)
    biases = vector_set[4 * D:8 * D].reshape(4, D)
    bias_up = vector_set[8 * D:8 * D + FF]
    bias_down = vector_set[8 * D + FF:9 * D + FF]
    label_table = vector_set[9 * D + FF:].reshape(4, D)
    return (norm_gains, biases, bias_up, bias_down, label_table)

def prompt_embed(label_ids, coord_ids, fourier, label_table):
    position = 2.0 * (coord_ids.astype(jnp.float32) + 0.5) / IMG - 1.0
    angles = 2.0 * math.pi * (position[:, 0:1] * fourier[0][None, :] + position[:, 1:2] * fourier[1][None, :])
    onehot = (label_ids[:, None] == jnp.arange(4, dtype=jnp.int32)[None, :]).astype(jnp.float32)
    return jnp.concatenate([jnp.sin(angles), jnp.cos(angles)], axis=1) + matmul(onehot, label_table)

def decoder_block(self_w, cross_w, mlp_w, vector_set, image_rows, label_ids, coord_ids, fourier):
    norm_gains, biases, bias_up, bias_down, label_table = unpack(vector_set)
    prompt = prompt_embed(label_ids, coord_ids, fourier, label_table)
    self_mixed = attention(to_heads(matmul(prompt, self_w[0])), to_heads(matmul(prompt, self_w[1])), to_heads(matmul(prompt, self_w[2])))
    after_self = layer_norm(prompt + matmul(from_heads(self_mixed), self_w[3]), norm_gains[0], biases[0])
    gathered = attention(to_heads(matmul(after_self, cross_w[0])), to_heads(matmul(image_rows, cross_w[1])), to_heads(matmul(image_rows, cross_w[2])))
    after_cross = layer_norm(after_self + matmul(from_heads(gathered), cross_w[3].T), norm_gains[1], biases[1])
    hidden = jax.nn.gelu(matmul(after_cross, mlp_w[0].T) + bias_up, approximate=False)
    after_mlp = layer_norm(after_cross + matmul(hidden, mlp_w[1]) + bias_down, norm_gains[2], biases[2])
    spread_back = attention(to_heads(matmul(image_rows, cross_w[4])), to_heads(matmul(after_mlp, cross_w[5])), to_heads(matmul(after_mlp, cross_w[6])))
    image_out = layer_norm(image_rows + matmul(from_heads(spread_back), cross_w[7].T), norm_gains[3], biases[3])
    return (after_mlp, image_out)

def newton_schulz(moment):
    matrix_norm = jnp.sqrt(lax.optimization_barrier(jnp.sum(moment * moment, axis=(1, 2))))
    ortho = moment / (matrix_norm[:, None, None] + SCALE_EPSILON)
    for sweep in range(NS_ITERS):
        gram_matrix = jnp.einsum('krc,krd->kcd', ortho, ortho, precision=HIGHEST)
        polynomial = COEF_CUBIC * gram_matrix + COEF_QUINTIC * jnp.einsum('kcd,kde->kce', gram_matrix, gram_matrix, precision=HIGHEST)
        ortho = COEF_LINEAR * ortho + jnp.einsum('krc,kcd->krd', ortho, polynomial, precision=HIGHEST)
    return ortho

def muon_update(weight, moment, gradient):
    new_moment = MOMENTUM_DECAY * moment + gradient
    ortho = newton_schulz(new_moment)
    step_rate = MATRIX_RATE * math.sqrt(weight.shape[1])
    return (new_moment, weight * (1.0 - MATRIX_RATE * MATRIX_DECAY) - step_rate * ortho)

def reference(image, labels, coords, fourier, self_weights, cross_weights, mlp_weights, vectors, query_cot, key_cot, self_moment, cross_moment, mlp_moment, vec_first, vec_second):

    def forward(self_w, cross_w, mlp_w, vector_set, image_all):

        def one_slice(items):
            return decoder_block(self_w, cross_w, mlp_w, vector_set, items[0], items[1], items[2], fourier)
        return lax.map(jax.checkpoint(one_slice), (image_all, labels, coords))
    results, pullback = jax.vjp(forward, self_weights, cross_weights, mlp_weights, vectors, image)
    grad_self, grad_cross, grad_mlp, grad_vector, image_grad = pullback((query_cot, key_cot))
    self_moment_new, self_new = muon_update(self_weights, self_moment, grad_self)
    cross_moment_new, cross_new = muon_update(cross_weights, cross_moment, grad_cross)
    mlp_moment_new, mlp_new = muon_update(mlp_weights, mlp_moment, grad_mlp)
    first_new = FIRST_DECAY * vec_first + (1.0 - FIRST_DECAY) * grad_vector
    second_new = SECOND_DECAY * vec_second + (1.0 - SECOND_DECAY) * grad_vector * grad_vector
    direction = first_new / (1.0 - FIRST_DECAY ** STEP) / (jnp.sqrt(second_new / (1.0 - SECOND_DECAY ** STEP)) + VECTOR_EPSILON)
    vectors_new = vectors - VECTOR_RATE * direction
    return (results[0], results[1], image_grad, self_moment_new, self_new, cross_moment_new, cross_new, mlp_moment_new, mlp_new, first_new, second_new, vectors_new)
```

```python
import functools
import math

import jax
import jax.numpy as jnp
from jax import lax
from jax.experimental import pallas as pl
from jax.experimental.pallas import tpu as pltpu
from jax.sharding import PartitionSpec as P

D = 256
HEADS = 8
CROSS = 128
FF = 2048
IMG = 1024
NS_ITERS = 5
STEP = 10
NORM_EPSILON = 1e-05
COEF_LINEAR = 3.4445
COEF_CUBIC = -4.775
COEF_QUINTIC = 2.0315
MOMENTUM_DECAY = 0.95
MATRIX_RATE = 0.05
MATRIX_DECAY = 0.01
SCALE_EPSILON = 1e-07
VECTOR_RATE = 0.1
FIRST_DECAY = 0.9
SECOND_DECAY = 0.999
VECTOR_EPSILON = 1e-08

MESH = pl.DeviceIdType.MESH
f32 = jnp.float32
HIGH = lax.Precision.HIGHEST
HIGHEST = lax.Precision.HIGHEST
SELF_SCALE = 1.0 / math.sqrt(D // HEADS)
CROSS_SCALE = 1.0 / math.sqrt(CROSS // HEADS)
CROSS_OF = ((4, 7), (2, 1), (0, 3), (5, 6))


def mm(a, b, dims, prec=HIGH):
    return lax.dot_general(a, b, (dims, ((), ())), precision=prec, preferred_element_type=f32)


def nn(a, b, prec=HIGH):
    return mm(a, b, ((1,), (0,)), prec)


def nt(a, b, prec=HIGH):
    return mm(a, b, ((1,), (1,)), prec)


def tn(a, b, prec=HIGH):
    return mm(a, b, ((0,), (0,)), prec)


def iota(shape, dim):
    return lax.broadcasted_iota(jnp.int32, shape, dim)


def head_mask(rows, width):
    shape = (HEADS * rows, width)
    return (lax.div(iota(shape, 0), rows) == lax.div(iota(shape, 1), width // HEADS)).astype(f32)


def expand(x, mask):
    return jnp.concatenate([x] * HEADS, axis=0) * mask


def extract(u, mask):
    rows = u.shape[0] // HEADS
    return (u * mask).reshape(HEADS, rows, u.shape[1]).sum(axis=0)


def normed(x):
    center = x - jnp.mean(x, axis=-1, keepdims=True)
    r = lax.rsqrt(jnp.mean(center * center, axis=-1, keepdims=True) + NORM_EPSILON)
    return center * r, r


def norm_back(dy, xhat, r, gain):
    t = dy * gain
    return (t - jnp.mean(t, axis=-1, keepdims=True) - xhat * jnp.mean(t * xhat, axis=-1, keepdims=True)) * r


def col_sum(x):
    return jnp.sum(x, axis=0, keepdims=True)


def row_of(vec, k):
    return jnp.concatenate([vec[2 * k : 2 * k + 1], vec[2 * k + 1 : 2 * k + 2]], axis=1)


def embed(pos, fourier, vec):
    px = 2.0 * (pos[:, 0:1] + 0.5) / IMG - 1.0
    py = 2.0 * (pos[:, 1:2] + 0.5) / IMG - 1.0
    label = pos[:, 2:3]
    angles = 2.0 * math.pi * (px * fourier[0:1] + py * fourier[1:2])
    out = jnp.concatenate([jnp.sin(angles), jnp.cos(angles)], axis=1)
    for k in range(4):
        out = out + jnp.where(label == float(k), row_of(vec, 17 + k), 0.0)
    return out


def front(prompt, sw, vec):
    rows = prompt.shape[0]
    mask = head_mask(rows, D)
    q, k, v = (nn(prompt, sw[i]) for i in range(3))
    qe = expand(q, mask)
    shape = (HEADS * rows, rows)
    of_row = lax.div(lax.rem(iota(shape, 0), rows), 8)
    of_col = lax.div(iota(shape, 1), 8)
    valid = (of_row == of_col) & (lax.rem(iota(shape, 1), 8) != 7)
    s = jnp.where(valid, nt(qe, k) * SELF_SCALE, -1e30)
    e = jnp.exp(s - jnp.max(s, axis=-1, keepdims=True))
    a = e / jnp.sum(e, axis=-1, keepdims=True)
    o = extract(nn(a, v), mask)
    xhat, r = normed(prompt + nn(o, sw[3]))
    after = xhat * row_of(vec, 0) + row_of(vec, 4)
    return after, (qe, k, v, a, o, xhat, r)


def gelu_parts(x):
    cdf = 0.5 * (1.0 + lax.erf(x * (1.0 / math.sqrt(2.0))))
    return x * cdf, cdf


def gelu_slope(x, cdf):
    return cdf + x * jnp.exp(-0.5 * x * x) * (1.0 / math.sqrt(2.0 * math.pi))


def pick(core, a, b):
    return jnp.where(core == 0, a, b)


def kernel(
    labels,
    coords,
    image,
    fourier,
    sw_in,
    cw_in,
    mw_in,
    vec_in,
    qc,
    kc,
    sm_in,
    cm_in,
    mm_in,
    out_q,
    out_k,
    out_ig,
    out_sm,
    out_sn,
    out_cm,
    out_cn,
    out_mm,
    out_mn,
    out_vec,
    image_v,
    fourier_v,
    sw,
    cw,
    mw,
    vec_v,
    qc_v,
    kc_v,
    moment_s,
    moment_c,
    moment_m,
    pos,
    c1_pair,
    c1_all,
    c2_pair,
    c2_all,
    c3_pair,
    c3_all,
    c3_z,
    grad_img,
    grad_pair,
    grad_rs,
    grad_z,
    grad_full,
    wide_z,
    small_z,
    front_v,
    s1_v,
    sc_x,
    ss_x,
    ig_v,
    in_sem,
    mom_sem,
    send_sem,
    recv_sem,
):
    seq = lax.axis_index("seq")
    opt = lax.axis_index("opt")
    core = lax.rem(seq, 2)
    chip = lax.div(seq, 2)
    sibling = {"seq": seq + 1 - 2 * core}

    def across(i):
        return {"seq": 2 * lax.rem(chip + i, 16) + core}

    def along(i):
        return {"opt": lax.rem(opt + i, 4)}

    def remote(src, dst, k, to):
        return pltpu.make_async_remote_copy(src, dst, send_sem.at[k], recv_sem.at[k], to, MESH)

    def wait_bytes(ref, sem):
        pltpu.make_async_copy(ref, ref, sem).wait()

    def pair_start(buf, k):
        remote(buf.at[core], buf.at[core], k, sibling).start()

    def pair_finish(buf, k):
        wait_bytes(buf.at[0], recv_sem.at[k])
        wait_bytes(buf.at[0], send_sem.at[k])

    def plane_start(buf, k):
        for i in range(1, 16):
            remote(buf.at[chip], buf.at[chip], k, across(i)).start()

    def plane_finish(buf, k):
        part = buf.at[pl.ds(0, 15)]
        wait_bytes(part, recv_sem.at[k])
        wait_bytes(part, send_sem.at[k])

    def z_start(buf, k):
        for i in range(1, 4):
            remote(buf.at[opt], buf.at[opt], k, along(i)).start()

    def z_finish(buf, k):
        part = buf.at[pl.ds(0, 3)]
        wait_bytes(part, recv_sem.at[k])
        wait_bytes(part, send_sem.at[k])

    def scatter_start(src, buf, k):
        for i in range(1, 16):
            to = lax.rem(chip + i, 16)
            remote(src.at[pl.ds(pl.multiple_of(to * 16, 16), 16)], buf.at[chip], k, across(i)).start()

    def gather_start(full, k):
        mine = full.at[pl.ds(pl.multiple_of(chip * 16, 16), 16)]
        for i in range(1, 16):
            remote(mine, mine, k, across(i)).start()

    def gather_finish(full, k):
        part = full.at[pl.ds(0, 240)]
        wait_bytes(part, recv_sem.at[k])
        wait_bytes(part, send_sem.at[k])

    loads = [
        pltpu.make_async_copy(src, dst, in_sem.at[i])
        for i, (src, dst) in enumerate(
            (
                (vec_in, vec_v),
                (fourier, fourier_v),
                (sw_in, sw),
                (cw_in, cw),
                (image, image_v),
                (mw_in, mw),
                (qc, qc_v),
                (kc, kc_v),
            )
        )
    ]
    for c in loads:
        c.start()

    barrier = pltpu.get_barrier_semaphore()
    peers = [sibling] + [across(i) for i in range(1, 16)] + [along(i) for i in range(1, 4)]
    for p in peers:
        pl.semaphore_signal(barrier, inc=1, device_id=p, device_id_type=MESH)

    lane = iota((16, 128), 1)
    row = iota((16, 128), 0)
    tile = jnp.zeros((16, 128), f32)
    for b in range(2):
        for i in range(7):
            here = row == 8 * b + i
            for c, value in enumerate((coords[b, 0, i], coords[b, 1, i], labels[b, i])):
                tile = jnp.where(here & (lane == c), value.astype(f32), tile)
    pos[opt] = tile
    pl.semaphore_wait(barrier, len(peers))

    z_start(pos, 0)
    mine_s = pl.ds(pl.multiple_of(opt * 64, 64), 64)
    mine_m = pl.ds(pl.multiple_of(opt * 512, 512), 512)
    cross_at = [a + (b - a) * core for a, b in CROSS_OF]
    parts = [(sm_in.at[pl.ds(2 * core, 2)], moment_s.at[:, mine_s], 0)]
    parts += [(cm_in.at[cross_at[j]], moment_c.at[j, mine_s], 1) for j in range(4)]
    parts += [(mm_in.at[core], moment_m.at[mine_m], 2)]
    for src, dst, k in parts:
        pltpu.make_async_copy(src, dst, mom_sem.at[k]).start()
        for i in range(1, 4):
            pltpu.make_async_remote_copy(src, dst, mom_sem.at[3 + k], mom_sem.at[6 + k], along(i), MESH).start()

    for c in loads[:4]:
        c.wait()
    vec = vec_v[...]
    after_self, _ = front(embed(pos[opt], fourier_v[...], vec), sw, vec)
    queries = nn(after_self, cw[0])

    loads[4].wait()
    mask64 = head_mask(8, CROSS)
    qe, qt = [], []
    o_parts, lse_parts = [], []
    for b in range(2):
        qe.append(expand(queries[8 * b : 8 * b + 8], mask64))
        qt.append(nt(qe[b], cw[1]))
        s = nt(qt[b], image_v[b]) * CROSS_SCALE
        s1_v[b] = s
        top = jnp.max(s, axis=-1, keepdims=True)
        e = jnp.exp(s - top)
        total = jnp.sum(e, axis=-1, keepdims=True)
        u = nn(e, image_v[b]) / total
        o_parts.append(extract(nn(u, cw[2]), mask64))
        lse_parts.append(extract(jnp.broadcast_to(top + jnp.log(total), (64, 128)), mask64))
    c1_pair[core] = jnp.concatenate(o_parts + lse_parts, axis=0)
    pair_start(c1_pair, 1)
    pair_finish(c1_pair, 1)

    def joined(buf):
        o, lse = buf[:, 0:16], buf[:, 16:32]
        top = jnp.max(lse, axis=0)
        w = jnp.exp(lse - top[None])
        total = jnp.sum(w, axis=0)
        return jnp.sum(w * o, axis=0) / total, top + jnp.log(total)

    c1_all[chip] = jnp.concatenate(joined(c1_pair), axis=0)
    plane_start(c1_all, 2)

    z_finish(pos, 0)
    prompt_all = embed(pos[...].reshape(64, 128), fourier_v[...], vec)
    after_all, (qe_s, k_s, v_s, a_s, o_s, xhat0, r0) = front(prompt_all, sw, vec)

    plane_finish(c1_all, 2)
    gathered, lse = joined(c1_all)

    xhat1, r1 = normed(after_self + nt(gathered, cw[3]))
    after_cross = xhat1 * row_of(vec, 1) + row_of(vec, 5)
    loads[5].wait()
    bias_up = jnp.concatenate([vec[16 + k : 17 + k] for k in range(16)], axis=1)
    hidden_in = nt(after_cross, mw[0]) + bias_up
    hidden, cdf = gelu_parts(hidden_in)
    xhat2, r2 = normed(after_cross + nn(hidden, mw[1]) + row_of(vec, 16))
    after_mlp = xhat2 * row_of(vec, 2) + row_of(vec, 6)
    for b in range(2):
        for i in range(7):
            out_q[i, b : b + 1] = after_mlp[8 * b + i : 8 * b + i + 1]
    prompt_keys = nn(after_mlp, cw[5])
    prompt_values = nn(after_mlp, cw[6])

    loads[7].wait()
    gain3, bias3 = row_of(vec, 3), row_of(vec, 7)
    real_row = lax.rem(iota((64, 128), 0), 8) != 7
    pke, pve, uq, uo = [], [], [], []
    dpk, dpv = [], []
    dg3 = jnp.zeros((1, D), f32)
    dc3 = jnp.zeros((1, D), f32)
    for b in range(2):
        img = image_v[b]
        pke.append(expand(prompt_keys[8 * b : 8 * b + 8], mask64))
        pve.append(expand(prompt_values[8 * b : 8 * b + 8], mask64))
        kt = nt(pke[b], cw[4])
        vt = nt(pve[b], cw[7])
        s = jnp.where(real_row, nt(kt, img) * CROSS_SCALE, -1e30).reshape(8, 8, 128)
        e = jnp.exp(s - jnp.max(s, axis=1, keepdims=True))
        a3 = e / jnp.sum(e, axis=1, keepdims=True)
        a = a3.reshape(64, 128)
        xhat3, r3 = normed(img + tn(a, vt))
        out_k[b] = xhat3 * gain3 + bias3
        dy = kc_v[b]
        dg3 = dg3 + col_sum(dy * xhat3)
        dc3 = dc3 + col_sum(dy)
        dx = norm_back(dy, xhat3, r3, gain3)
        da = nt(vt, dx).reshape(8, 8, 128)
        ds = (a3 * (da - jnp.sum(a3 * da, axis=1, keepdims=True)) * CROSS_SCALE).reshape(64, 128)
        ig_v[b] = dx + tn(ds, kt)
        uq.append(nn(ds, img))
        uo.append(nn(a, dx))
        dpk.append(extract(nn(uq[b], cw[4]), mask64))
        dpv.append(extract(nn(uo[b], cw[7]), mask64))
    fill = row == 7
    fill2 = row == 15

    def with_rows(x, first, second):
        return jnp.where(fill, first, jnp.where(fill2, second, x))

    c2_pair[core] = jnp.concatenate(
        [
            with_rows(jnp.concatenate(dpk, axis=0), dg3[:, :128], dg3[:, 128:]),
            with_rows(jnp.concatenate(dpv, axis=0), dc3[:, :128], dc3[:, 128:]),
        ],
        axis=0,
    )
    pair_start(c2_pair, 3)
    grad_img[0, 0] = tn(uq[0], pke[0]) + tn(uq[1], pke[1])
    grad_img[0, 1] = tn(uo[0], pve[0]) + tn(uo[1], pve[1])
    pair_finish(c2_pair, 3)
    c2_all[chip] = c2_pair[0] + c2_pair[1]
    plane_start(c2_all, 4)

    def pair_grad_start(t, k):
        remote(grad_img.at[t, 1 - core], grad_pair.at[t], k, sibling).start()

    def pair_grad_finish(t, k):
        wait_bytes(grad_pair.at[t], recv_sem.at[k])
        wait_bytes(grad_pair.at[t], send_sem.at[k])
        grad_pair[t] = grad_img[t, core] + grad_pair[t]

    own_chunk = pl.ds(pl.multiple_of(chip * 16, 16), 16)

    def scatter_finish(t, k):
        plane_finish(grad_rs.at[t], k)
        grad_rs[t, chip] = grad_pair[t, own_chunk]
        grad_z[t, opt] = jnp.sum(grad_rs[t], axis=0)

    def z_grad_finish(t, k):
        z_finish(grad_z.at[t], k)
        grad_full[t, own_chunk] = jnp.sum(grad_z[t], axis=0)

    pair_grad_start(0, 5)
    pair_grad_finish(0, 5)
    scatter_start(grad_pair.at[0], grad_rs.at[0], 6)

    loads[6].wait()
    filler = jnp.zeros((1, D), f32)
    query_cot = jnp.concatenate(
        [qc_v[i, b : b + 1] if i < 7 else filler for b in range(2) for i in range(8)], axis=0
    )
    plane_finish(c2_all, 4)
    c2 = jnp.sum(c2_all[...], axis=0)
    keep = ((row != 7) & (row != 15)).astype(f32)
    dpk_sum = c2[0:16] * keep
    dpv_sum = c2[16:32] * keep
    dg3 = jnp.concatenate([c2[7:8], c2[15:16]], axis=1)
    dc3 = jnp.concatenate([c2[23:24], c2[31:32]], axis=1)

    d_mlp = query_cot + nt(dpk_sum, cw[5]) + nt(dpv_sum, cw[6])
    dg2, dc2 = col_sum(d_mlp * xhat2), col_sum(d_mlp)
    d2 = norm_back(d_mlp, xhat2, r2, row_of(vec, 2))
    d_hidden = nt(d2, mw[1]) * gelu_slope(hidden_in, cdf)
    d_cross = d2 + nn(d_hidden, mw[0])
    dg1, dc1 = col_sum(d_cross * xhat1), col_sum(d_cross)
    d1 = norm_back(d_cross, xhat1, r1, row_of(vec, 1))
    d_gathered = nn(d1, cw[3])

    wide_z[opt] = pick(core, d_hidden, hidden)
    z_start(wide_z, 7)
    db_up = col_sum(d_hidden)
    vec_rows = [dg1, dg2, dg3, dc1, dc2, dc3, col_sum(d2), filler]
    vec_rows += [db_up[:, 256 * k : 256 * k + 256] for k in range(8)]
    small_z[opt] = jnp.concatenate(
        [
            d1,
            after_mlp,
            pick(core, after_cross, d2),
            jnp.concatenate([gathered, pick(core, dpk_sum, dpv_sum)], axis=1),
            jnp.concatenate(vec_rows, axis=0),
        ],
        axis=0,
    )
    z_start(small_z, 8)
    scatter_finish(0, 6)
    z_start(grad_z.at[0], 9)

    pick_lane = (iota((64, 128), 1) == lax.div(iota((64, 128), 0), 8) * 16).astype(f32)
    dge, gt, uk, uv, dq = [], [], [], [], []
    for b in range(2):
        img = image_v[b]
        rows8 = slice(8 * b, 8 * b + 8)
        dge.append(expand(d_gathered[rows8], mask64))
        gt = nt(dge[b], cw[2])
        lse_col = jnp.sum(jnp.concatenate([lse[rows8]] * 8, axis=0) * pick_lane, axis=-1, keepdims=True)
        p = jnp.exp(s1_v[b] - lse_col)
        dot = jnp.sum(dge[b] * jnp.concatenate([gathered[rows8]] * 8, axis=0), axis=-1, keepdims=True)
        ds = p * (nt(gt, img) - dot) * CROSS_SCALE
        uk.append(nn(ds, img))
        uv.append(nn(p, img))
        dq.append(extract(nn(uk[b], cw[1]), mask64))
        ig_v[b] = ig_v[b] + tn(ds, qt[b]) + tn(p, gt)
    c3_pair[core] = jnp.concatenate(dq, axis=0)
    pair_start(c3_pair, 10)
    grad_img[1, 0] = tn(uv[0], dge[0]) + tn(uv[1], dge[1])
    grad_img[1, 1] = tn(uk[0], qe[0]) + tn(uk[1], qe[1])
    pair_finish(c3_pair, 10)
    c3_all[chip] = c3_pair[0] + c3_pair[1]
    plane_start(c3_all, 11)
    pair_grad_start(1, 12)
    pair_grad_finish(1, 12)
    scatter_start(grad_pair.at[1], grad_rs.at[1], 13)
    out_ig[...] = ig_v[...]

    z_grad_finish(0, 9)
    gather_start(grad_full.at[0], 14)

    plane_finish(c3_all, 11)
    c3_z[opt] = jnp.sum(c3_all[...], axis=0)
    z_start(c3_z, 15)
    scatter_finish(1, 13)
    z_start(grad_z.at[1], 16)

    for src, dst, k in parts:
        pltpu.make_async_copy(src, dst, mom_sem.at[k]).wait()
    for buf, k in ((moment_s.at[:, pl.ds(0, 192)], 0), (moment_c.at[:, pl.ds(0, 192)], 1), (moment_m.at[pl.ds(0, 1536)], 2)):
        wait_bytes(buf, mom_sem.at[3 + k])
        wait_bytes(buf, mom_sem.at[6 + k])
    z_finish(wide_z, 7)
    z_finish(small_z, 8)
    small = small_z[...]
    d1_all = small[:, 0:16].reshape(64, D)
    mlp_all = small[:, 16:32].reshape(64, D)
    narrow_all = small[:, 32:48].reshape(64, D)
    pair_all = small[:, 48:64].reshape(64, D)
    vec_sum = jnp.sum(small[:, 64:80], axis=0)
    m_new = MOMENTUM_DECAY * moment_m[...] + tn(wide_z[...].reshape(64, FF), narrow_all)
    moment_m[...] = m_new
    scale_m = 1.0 / (jnp.sqrt(jnp.sum(m_new * m_new)) + SCALE_EPSILON)
    gram = tn(m_new, m_new, HIGHEST) * (scale_m * scale_m)
    eye = (iota((D, D), 0) == iota((D, D), 1)).astype(f32)
    total = None
    for sweep in range(NS_ITERS):
        poly = COEF_LINEAR * eye + COEF_CUBIC * gram + COEF_QUINTIC * nn(gram, gram, HIGHEST)
        total = poly if total is None else nn(total, poly, HIGHEST)
        if sweep + 1 < NS_ITERS:
            gram = nn(nn(poly, gram, HIGHEST), poly, HIGHEST)
    own_m = moment_m[mine_m]
    out_mm[core] = own_m
    decay = 1.0 - MATRIX_RATE * MATRIX_DECAY
    out_mn[core] = decay * mw[core, mine_m] - (MATRIX_RATE * math.sqrt(FF)) * nn(own_m * scale_m, total)
    remote(out_mm.at[core], out_mm.at[core], 17, sibling).start()
    remote(out_mn.at[core], out_mn.at[core], 18, sibling).start()

    z_finish(c3_z, 15)
    dq_all = c3_z[...].reshape(64, CROSS)
    z_grad_finish(1, 16)
    gather_start(grad_full.at[1], 19)
    d_after = d1_all + nt(dq_all, cw[0])
    dg0, dc0 = col_sum(d_after * xhat0), col_sum(d_after)
    d0 = norm_back(d_after, xhat0, r0, row_of(vec, 0))
    mask512 = head_mask(64, D)
    doe = expand(nt(d0, sw[3]), mask512)
    da = nt(doe, v_s)
    ds = a_s * (da - jnp.sum(a_s * da, axis=-1, keepdims=True)) * SELF_SCALE
    dq_s = extract(nn(ds, k_s), mask512)
    dk_s = tn(ds, qe_s)
    dv_s = tn(a_s, doe)
    d_prompt = d0 + nt(dq_s, sw[0]) + nt(dk_s, sw[1]) + nt(dv_s, sw[2])
    label_all = pos[...].reshape(64, 128)[:, 2:3]
    d_label = [col_sum(jnp.where(label_all == float(k), d_prompt, 0.0)) for k in range(4)]

    norm_rows = [dg0] + [vec_sum[k : k + 1] for k in range(3)] + [dc0] + [vec_sum[k : k + 1] for k in range(3, 6)]
    vec_all = norm_rows + [vec_sum[8 + k : 9 + k] for k in range(8)] + [vec_sum[6:7]] + d_label
    for k, line in enumerate(vec_all):
        out_vec[2 * k : 2 * k + 1] = line[:, :128]
        out_vec[2 * k + 1 : 2 * k + 2] = line[:, 128:]

    first = tn(prompt_all, pick(core, dq_s, dv_s))
    second = tn(pick(core, prompt_all, o_s), pick(core, dk_s, d0))
    third = tn(pick(core, after_all, d1_all), pick(core, dq_all, pair_all[:, :128]))
    fourth = tn(mlp_all, pair_all[:, 128:])
    gather_finish(grad_full.at[0], 14)
    gather_finish(grad_full.at[1], 19)
    self_m = [MOMENTUM_DECAY * moment_s[j] + g for j, g in enumerate((first, second))]
    cross_m = [MOMENTUM_DECAY * moment_c[j] + g for j, g in enumerate((grad_full[0], grad_full[1], third, fourth))]
    for j in range(2):
        moment_s[j] = self_m[j]
        out_sm[2 * core + j] = moment_s[j, mine_s]
    for j in range(4):
        moment_c[j] = cross_m[j]
        out_cm[cross_at[j]] = moment_c[j, mine_s]
    own_s = pl.ds(2 * core, 2)
    remote(out_sm.at[own_s], out_sm.at[own_s], 20, sibling).start()
    for j in range(4):
        remote(out_cm.at[cross_at[j]], out_cm.at[cross_at[j]], 21, sibling).start()

    xs = [m * (1.0 / (jnp.sqrt(jnp.sum(m * m)) + SCALE_EPSILON)) for m in self_m + cross_m]
    for sweep in range(NS_ITERS):
        grams = [tn(x, x) for x in xs]
        polys = [COEF_CUBIC * g + COEF_QUINTIC * nn(g, g) for g in grams]
        if sweep + 1 == NS_ITERS:
            for j in range(2):
                ss_x[j] = xs[j]
            for j in range(4):
                sc_x[j] = xs[2 + j]
            xs = [ss_x[j, mine_s] for j in range(2)] + [sc_x[j, mine_s] for j in range(4)]
        xs = [COEF_LINEAR * x + nn(x, p) for x, p in zip(xs, polys)]
    rate = MATRIX_RATE * math.sqrt(D)
    for j in range(2):
        out_sn[2 * core + j] = decay * sw[2 * core + j, mine_s] - rate * xs[j]
    for j in range(4):
        out_cn[cross_at[j]] = decay * cw[cross_at[j], mine_s] - rate * xs[2 + j]
    remote(out_sn.at[own_s], out_sn.at[own_s], 22, sibling).start()
    for j in range(4):
        remote(out_cn.at[cross_at[j]], out_cn.at[cross_at[j]], 23, sibling).start()

    for buf, k in (
        (out_mm.at[0], 17),
        (out_mn.at[0], 18),
        (out_sm.at[pl.ds(0, 2)], 20),
        (out_cm.at[pl.ds(0, 4)], 21),
        (out_sn.at[pl.ds(0, 2)], 22),
        (out_cn.at[pl.ds(0, 4)], 23),
    ):
        wait_bytes(buf, recv_sem.at[k])
        wait_bytes(buf, send_sem.at[k])


N_EXCHANGES = 24


def finish_kernel(*refs):
    n = len(refs) // 2
    for src, dst in zip(refs[:n], refs[n:]):
        dst[...] = src[...]


def per_device(
    image,
    labels,
    coords,
    fourier,
    self_weights,
    cross_weights,
    mlp_weights,
    vectors,
    query_cot,
    key_cot,
    self_moment,
    cross_moment,
    mlp_moment,
    vec_first,
    vec_second,
):
    sds = lambda *s: jax.ShapeDtypeStruct(s, f32)
    out_shape = [
        sds(7, 2, 256),
        sds(2, 128, 256),
        sds(2, 128, 256),
        sds(4, 64, 256),
        sds(4, 64, 256),
        sds(8, 64, 128),
        sds(8, 64, 128),
        sds(2, 512, 256),
        sds(2, 512, 256),
        sds(42, 128),
    ]
    whole = pl.BlockSpec(memory_space=pl.ANY)
    inside = pl.BlockSpec(memory_space=pltpu.VMEM)
    scalars = pl.BlockSpec(memory_space=pltpu.SMEM)
    dma = pltpu.SemaphoreType.DMA
    v = lambda *s: pltpu.VMEM(s, f32)
    results = pl.pallas_call(
        kernel,
        out_shape=out_shape,
        in_specs=[scalars, scalars] + [whole] * 11,
        out_specs=[inside] * len(out_shape),
        scratch_shapes=[
            v(2, 128, 256),
            v(2, 128),
            v(4, 256, 256),
            v(8, 256, 128),
            v(2, 2048, 256),
            v(42, 128),
            v(7, 2, 256),
            v(2, 128, 256),
            v(2, 256, 256),
            v(4, 256, 128),
            v(2048, 256),
            v(4, 16, 128),
            v(2, 32, 128),
            v(16, 32, 128),
            v(2, 32, 128),
            v(16, 32, 128),
            v(2, 16, 128),
            v(16, 16, 128),
            v(4, 16, 128),
            v(2, 2, 256, 128),
            v(2, 256, 128),
            v(2, 16, 16, 128),
            v(2, 4, 16, 128),
            v(2, 256, 128),
            v(4, 16, 2048),
            v(4, 80, 256),
            v(8, 128),
            v(2, 64, 128),
            v(4, 256, 128),
            v(2, 256, 256),
            v(2, 128, 256),
            dma((8,)),
            dma((9,)),
            dma((N_EXCHANGES,)),
            dma((N_EXCHANGES,)),
        ],
        compiler_params=pltpu.CompilerParams(
            collective_id=0, has_side_effects=True, vmem_limit_bytes=60 * 2**20
        ),
    )(
        labels,
        coords.transpose(0, 2, 1),
        image,
        fourier,
        self_weights,
        cross_weights,
        mlp_weights,
        vectors.reshape(42, 128),
        query_cot.transpose(1, 0, 2),
        key_cot,
        self_moment,
        cross_moment,
        mlp_moment,
    )
    done = pl.pallas_call(
        finish_kernel,
        out_shape=out_shape[:9],
        in_specs=[inside] * 9,
        out_specs=[inside] * 9,
        compiler_params=pltpu.CompilerParams(vmem_limit_bytes=60 * 2**20),
    )(*results[:9])
    share = vec_first.shape[0]
    at = lax.axis_index("opt") * share
    grad = lax.dynamic_slice_in_dim(results[9].reshape(-1), at, share, 0)
    local = lax.dynamic_slice_in_dim(vectors, at, share, 0)
    first = FIRST_DECAY * vec_first + (1.0 - FIRST_DECAY) * grad
    second = SECOND_DECAY * vec_second + (1.0 - SECOND_DECAY) * grad * grad
    direction = (
        first
        / (1.0 - FIRST_DECAY**STEP)
        / (jnp.sqrt(second / (1.0 - SECOND_DECAY**STEP)) + VECTOR_EPSILON)
    )
    return (
        done[0].transpose(1, 0, 2),
        *done[1:],
        first,
        second,
        local - VECTOR_RATE * direction,
    )


def solution(mesh):
    in_specs = (
        P("opt", "seq", None),
        P("opt", None),
        P("opt", None, None),
        P(),
        P(),
        P(),
        P(),
        P(),
        P("opt", None, None),
        P("opt", "seq", None),
        P(None, "opt", None),
        P(None, "opt", None),
        P(None, "opt", None),
        P("opt"),
        P("opt"),
    )
    out_specs = (
        P("opt", None, None),
        P("opt", "seq", None),
        P("opt", "seq", None),
        P(None, "opt", None),
        P(None, "opt", None),
        P(None, "opt", None),
        P(None, "opt", None),
        P(None, "opt", None),
        P(None, "opt", None),
        P("opt"),
        P("opt"),
        P("opt"),
    )
    return jax.shard_map(
        per_device, mesh=mesh, in_specs=in_specs, out_specs=out_specs, check_vma=False
    )
```

```python
import functools
import math

import jax
import jax.numpy as jnp
from jax import lax
from jax.experimental import pallas as pl
from jax.experimental.pallas import tpu as pltpu
from jax.sharding import PartitionSpec as P

D = 256
HEADS = 8
CROSS = 128
FF = 2048
IMG = 1024
NS_ITERS = 5
STEP = 10
NORM_EPSILON = 1e-05
COEF_LINEAR = 3.4445
COEF_CUBIC = -4.775
COEF_QUINTIC = 2.0315
MOMENTUM_DECAY = 0.95
MATRIX_RATE = 0.05
MATRIX_DECAY = 0.01
SCALE_EPSILON = 1e-07
VECTOR_RATE = 0.1
FIRST_DECAY = 0.9
SECOND_DECAY = 0.999
VECTOR_EPSILON = 1e-08

MESH = pl.DeviceIdType.MESH
f32 = jnp.float32
HIGH = lax.Precision.HIGH
HIGHEST = lax.Precision.HIGHEST
P_FRONT = HIGHEST
P_SCORE = HIGHEST
P_MID = HIGH
P_BACK = HIGH
P_MIDB = HIGH
P_SCOREB = HIGH
P_FRONTB = HIGH
P_GRAD = HIGH
P_SWEEP = HIGH
SELF_SCALE = 1.0 / math.sqrt(D // HEADS)
CROSS_SCALE = 1.0 / math.sqrt(CROSS // HEADS)
CROSS_OF = ((4, 7), (2, 1), (0, 3), (5, 6))


def mm(a, b, dims, prec):
    return lax.dot_general(a, b, (dims, ((), ())), precision=prec, preferred_element_type=f32)


def nn(a, b, prec):
    return mm(a, b, ((1,), (0,)), prec)


def nt(a, b, prec):
    return mm(a, b, ((1,), (1,)), prec)


def tn(a, b, prec):
    return mm(a, b, ((0,), (0,)), prec)


def iota(shape, dim):
    return lax.broadcasted_iota(jnp.int32, shape, dim)


def head_mask(rows, width):
    shape = (HEADS * rows, width)
    return (lax.div(iota(shape, 0), rows) == lax.div(iota(shape, 1), width // HEADS)).astype(f32)


def expand(x, mask):
    return jnp.concatenate([x] * HEADS, axis=0) * mask


def extract(u, mask):
    rows = u.shape[0] // HEADS
    return (u * mask).reshape(HEADS, rows, u.shape[1]).sum(axis=0)


def normed(x):
    center = x - jnp.mean(x, axis=-1, keepdims=True)
    r = lax.rsqrt(jnp.mean(center * center, axis=-1, keepdims=True) + NORM_EPSILON)
    return center * r, r


def norm_back(dy, xhat, r, gain):
    t = dy * gain
    return (t - jnp.mean(t, axis=-1, keepdims=True) - xhat * jnp.mean(t * xhat, axis=-1, keepdims=True)) * r


def col_sum(x):
    return jnp.sum(x, axis=0, keepdims=True)


def row_of(vec, k):
    return jnp.concatenate([vec[2 * k : 2 * k + 1], vec[2 * k + 1 : 2 * k + 2]], axis=1)


def embed(pos, fourier, vec):
    px = 2.0 * (pos[:, 0:1] + 0.5) / IMG - 1.0
    py = 2.0 * (pos[:, 1:2] + 0.5) / IMG - 1.0
    label = pos[:, 2:3]
    angles = 2.0 * math.pi * (px * fourier[0:1] + py * fourier[1:2])
    out = jnp.concatenate([jnp.sin(angles), jnp.cos(angles)], axis=1)
    for k in range(4):
        out = out + jnp.where(label == float(k), row_of(vec, 17 + k), 0.0)
    return out


def front(prompt, sw, vec):
    rows = prompt.shape[0]
    mask = head_mask(rows, D)
    q, k, v = (nn(prompt, sw[i], P_FRONT) for i in range(3))
    qe = expand(q, mask)
    shape = (HEADS * rows, rows)
    of_row = lax.div(lax.rem(iota(shape, 0), rows), 8)
    of_col = lax.div(iota(shape, 1), 8)
    valid = (of_row == of_col) & (lax.rem(iota(shape, 1), 8) != 7)
    s = jnp.where(valid, nt(qe, k, P_FRONT) * SELF_SCALE, -1e30)
    e = jnp.exp(s - jnp.max(s, axis=-1, keepdims=True))
    a = e / jnp.sum(e, axis=-1, keepdims=True)
    o = extract(nn(a, v, P_FRONT), mask)
    xhat, r = normed(prompt + nn(o, sw[3], P_FRONT))
    after = xhat * row_of(vec, 0) + row_of(vec, 4)
    return after, (qe, k, v, a, o, xhat, r)


def gelu_parts(x):
    cdf = 0.5 * (1.0 + lax.erf(x * (1.0 / math.sqrt(2.0))))
    return x * cdf, cdf


def gelu_slope(x, cdf):
    return cdf + x * jnp.exp(-0.5 * x * x) * (1.0 / math.sqrt(2.0 * math.pi))


def pick(core, a, b):
    return jnp.where(core == 0, a, b)


def kernel(
    labels,
    coords,
    image,
    fourier,
    sw_in,
    cw_in,
    mw_in,
    vec_in,
    qc,
    kc,
    sm_in,
    cm_in,
    mm_in,
    out_q,
    out_k,
    out_ig,
    out_sm,
    out_sn,
    out_cm,
    out_cn,
    out_mm,
    out_mn,
    out_vec,
    image_v,
    fourier_v,
    sw,
    cw,
    mw,
    vec_v,
    qc_v,
    kc_v,
    moment_s,
    moment_c,
    moment_m,
    pos,
    c1_pair,
    c1_all,
    c2_pair,
    c2_all,
    c3_pair,
    c3_all,
    c3_z,
    grad_img,
    grad_pair,
    grad_rs,
    grad_z,
    grad_full,
    wide_z,
    early_z,
    narrow_z,
    small_z,
    s1_v,
    last_x,
    ig_v,
    in_sem,
    mom_sem,
    send_sem,
    recv_sem,
):
    seq = lax.axis_index("seq")
    opt = lax.axis_index("opt")
    core = lax.rem(seq, 2)
    chip = lax.div(seq, 2)
    sibling = {"seq": seq + 1 - 2 * core}

    def across(i):
        return {"seq": 2 * lax.rem(chip + i, 16) + core}

    def along(i):
        return {"opt": lax.rem(opt + i, 4)}

    def remote(src, dst, k, to):
        return pltpu.make_async_remote_copy(src, dst, send_sem.at[k], recv_sem.at[k], to, MESH)

    def finish(ref, k):
        pltpu.make_async_copy(ref, ref, recv_sem.at[k]).wait()
        pltpu.make_async_copy(ref, ref, send_sem.at[k]).wait()

    def pair_start(buf, k):
        remote(buf.at[core], buf.at[core], k, sibling).start()

    def pair_finish(buf, k):
        finish(buf.at[0], k)

    def plane_start(buf, k):
        for i in range(1, 16):
            remote(buf.at[chip], buf.at[chip], k, across(i)).start()

    def plane_finish(buf, k):
        part = buf.at[pl.ds(0, 15)]
        finish(part, k)

    def z_start(buf, k):
        for i in range(1, 4):
            remote(buf.at[opt], buf.at[opt], k, along(i)).start()

    def z_finish(buf, k):
        part = buf.at[pl.ds(0, 3)]
        finish(part, k)

    def scatter_start(src, buf, k):
        for i in range(1, 16):
            to = lax.rem(chip + i, 16)
            remote(src.at[pl.ds(pl.multiple_of(to * 16, 16), 16)], buf.at[chip], k, across(i)).start()

    def gather_start(full, k):
        mine = full.at[pl.ds(pl.multiple_of(chip * 16, 16), 16)]
        for i in range(1, 16):
            remote(mine, mine, k, across(i)).start()

    def gather_finish(full, k):
        part = full.at[pl.ds(0, 240)]
        finish(part, k)

    barrier = pltpu.get_barrier_semaphore()
    peers = [sibling] + [across(i) for i in range(1, 16)] + [along(i) for i in range(1, 4)]
    for p in peers:
        pl.semaphore_signal(barrier, inc=1, device_id=p, device_id_type=MESH)
    loads = [
        pltpu.make_async_copy(src, dst, in_sem.at[i])
        for i, (src, dst) in enumerate(
            (
                (vec_in, vec_v),
                (fourier, fourier_v),
                (sw_in, sw),
                (cw_in, cw),
                (image, image_v),
                (mw_in, mw),
                (qc, qc_v),
                (kc, kc_v),
            )
        )
    ]
    for c in loads:
        c.start()

    lane = iota((16, 128), 1)
    row = iota((16, 128), 0)
    tile = jnp.zeros((16, 128), f32)
    for b in range(2):
        for i in range(7):
            here = row == 8 * b + i
            for c, value in enumerate((coords[b, 0, i], coords[b, 1, i], labels[b, i])):
                tile = jnp.where(here & (lane == c), value.astype(f32), tile)
    pos[opt] = tile

    for c in loads[:4]:
        c.wait()
    vec = vec_v[...]
    after_self, _ = front(embed(tile, fourier_v[...], vec), sw, vec)
    queries = nn(after_self, cw[0], P_FRONT)

    pl.semaphore_wait(barrier, len(peers))

    z_start(pos, 0)
    mine_s = pl.ds(pl.multiple_of(opt * 64, 64), 64)
    mine_m = pl.ds(pl.multiple_of(opt * 512, 512), 512)
    cross_at = [a + (b - a) * core for a, b in CROSS_OF]
    parts = [(mm_in.at[core], moment_m.at[mine_m], 0)]
    parts += [(sm_in.at[pl.ds(2 * core, 2)], moment_s.at[:, mine_s], 1)]
    parts += [(cm_in.at[cross_at[j]], moment_c.at[j, mine_s], 2) for j in range(4)]
    for src, dst, k in parts:
        pltpu.make_async_copy(src, dst, mom_sem.at[k]).start()
        remote(src, dst, 24 + k, along(1)).start()
        remote(src, dst, 24 + k, along(3)).start()

    def rows_from(i, rows, half):
        start = lax.rem(opt + i, 4) * rows + half * (rows // 2)
        return pl.ds(pl.multiple_of(start, rows // 2), rows // 2)

    def pass_on(k):
        for i, half, to in ((3, 0, 1), (1, 1, 3)):
            if k == 0:
                views = [moment_m.at[rows_from(i, 512, half)]]
            elif k == 1:
                views = [moment_s.at[:, rows_from(i, 64, half)]]
            else:
                views = [moment_c.at[:, rows_from(i, 64, half)]]
            for view in views:
                remote(view, view, 27 + k, along(to)).start()

    first_moments = (moment_m.at[pl.ds(0, 1024)], moment_s.at[:, pl.ds(0, 128)], moment_c.at[:, pl.ds(0, 128)])
    last_moments = (moment_m.at[pl.ds(0, 512)], moment_s.at[:, pl.ds(0, 64)], moment_c.at[:, pl.ds(0, 64)])

    loads[4].wait()
    two = range(2)
    mask64 = head_mask(8, CROSS)

    def rows_of(x, b):
        return x[8 * b : 8 * b + 8]

    qe = [expand(rows_of(queries, b), mask64) for b in two]
    qt = [nt(qe[b], cw[1], P_SCORE) for b in two]
    s = [nt(qt[b], image_v[b], P_SCORE) * CROSS_SCALE for b in two]
    top = [jnp.max(s[b], axis=-1, keepdims=True) for b in two]
    e = [jnp.exp(s[b] - top[b]) for b in two]
    total = [jnp.sum(e[b], axis=-1, keepdims=True) for b in two]
    u = [nn(e[b], image_v[b], P_SCORE) / total[b] for b in two]
    o_parts = [extract(nn(u[b], cw[2], P_SCORE), mask64) for b in two]
    lse_parts = [extract(jnp.broadcast_to(top[b] + jnp.log(total[b]), (64, 128)), mask64) for b in two]
    for b in two:
        s1_v[b] = s[b]
    c1_pair[core] = jnp.concatenate(o_parts + lse_parts, axis=0)
    pair_start(c1_pair, 1)

    def joined(buf):
        o, lse = buf[:, 0:16], buf[:, 16:32]
        top = jnp.max(lse, axis=0)
        w = jnp.exp(lse - top[None])
        total = jnp.sum(w, axis=0)
        return jnp.sum(w * o, axis=0) / total, top + jnp.log(total)

    pair_finish(c1_pair, 1)
    c1_all[chip] = jnp.concatenate(joined(c1_pair), axis=0)
    plane_start(c1_all, 2)

    z_finish(pos, 0)
    prompt_all = embed(pos[...].reshape(64, 128), fourier_v[...], vec)
    after_all, (qe_s, k_s, v_s, a_s, o_s, xhat0, r0) = front(prompt_all, sw, vec)

    plane_finish(c1_all, 2)
    gathered, lse = joined(c1_all)

    xhat1, r1 = normed(after_self + nt(gathered, cw[3], P_MID))
    after_cross = xhat1 * row_of(vec, 1) + row_of(vec, 5)
    loads[5].wait()
    bias_up = jnp.concatenate([vec[16 + k : 17 + k] for k in range(16)], axis=1)
    hidden_in = nt(after_cross, mw[0], P_MID) + bias_up
    hidden, cdf = gelu_parts(hidden_in)
    xhat2, r2 = normed(after_cross + nn(hidden, mw[1], P_MID) + row_of(vec, 16))
    after_mlp = xhat2 * row_of(vec, 2) + row_of(vec, 6)
    for b in two:
        for i in range(7):
            out_q[i, b : b + 1] = after_mlp[8 * b + i : 8 * b + i + 1]
    prompt_keys = nn(after_mlp, cw[5], P_MID)
    prompt_values = nn(after_mlp, cw[6], P_MID)
    wide_z[1, opt] = hidden
    early_z[opt] = jnp.concatenate([after_mlp, after_cross], axis=0)
    @pl.when(core == 1)
    def _():
        z_start(wide_z.at[1], 7)

    z_start(early_z, 8)

    loads[7].wait()
    gain3, bias3 = row_of(vec, 3), row_of(vec, 7)
    real_row = lax.rem(iota((64, 128), 0), 8) != 7
    pke = [expand(rows_of(prompt_keys, b), mask64) for b in two]
    pve = [expand(rows_of(prompt_values, b), mask64) for b in two]
    kt = [nt(pke[b], cw[4], P_BACK) for b in two]
    vt = [nt(pve[b], cw[7], P_BACK) for b in two]
    s = [nt(kt[b], image_v[b], P_BACK) * CROSS_SCALE for b in two]
    s = [jnp.where(real_row, s[b], -1e30).reshape(8, 8, 128) for b in two]
    e = [jnp.exp(s[b] - jnp.max(s[b], axis=1, keepdims=True)) for b in two]
    a3 = [e[b] / jnp.sum(e[b], axis=1, keepdims=True) for b in two]
    a = [a3[b].reshape(64, 128) for b in two]
    n3 = [normed(image_v[b] + tn(a[b], vt[b], P_BACK)) for b in two]
    dx = [norm_back(kc_v[b], n3[b][0], n3[b][1], gain3) for b in two]
    da = [nt(vt[b], dx[b], P_BACK).reshape(8, 8, 128) for b in two]
    ds = [
        (a3[b] * (da[b] - jnp.sum(a3[b] * da[b], axis=1, keepdims=True)) * CROSS_SCALE).reshape(64, 128)
        for b in two
    ]
    uq = [nn(ds[b], image_v[b], P_BACK) for b in two]
    uo = [nn(a[b], dx[b], P_BACK) for b in two]
    dpk = [extract(nn(uq[b], cw[4], P_BACK), mask64) for b in two]
    dpv = [extract(nn(uo[b], cw[7], P_BACK), mask64) for b in two]
    dg3 = sum(col_sum(kc_v[b] * n3[b][0]) for b in two)
    dc3 = sum(col_sum(kc_v[b]) for b in two)
    fill = row == 7
    fill2 = row == 15

    def with_rows(x, first, second):
        return jnp.where(fill, first, jnp.where(fill2, second, x))

    c2_pair[core] = jnp.concatenate(
        [
            with_rows(jnp.concatenate(dpk, axis=0), dg3[:, :128], dg3[:, 128:]),
            with_rows(jnp.concatenate(dpv, axis=0), dc3[:, :128], dc3[:, 128:]),
        ],
        axis=0,
    )
    pair_start(c2_pair, 3)
    for b in two:
        out_k[b] = n3[b][0] * gain3 + bias3
    pair_finish(c2_pair, 3)
    c2_all[chip] = c2_pair[0] + c2_pair[1]
    plane_start(c2_all, 4)

    def pair_grad_start(t, k):
        remote(grad_img.at[t, 1 - core], grad_pair.at[t], k, sibling).start()

    def pair_grad_finish(t, k):
        finish(grad_pair.at[t], k)
        grad_pair[t] = grad_img[t, core] + grad_pair[t]

    own_chunk = pl.ds(pl.multiple_of(chip * 16, 16), 16)

    def scatter_finish(t, k):
        plane_finish(grad_rs.at[t], k)
        grad_rs[t, chip] = grad_pair[t, own_chunk]
        grad_z[t, opt] = jnp.sum(grad_rs[t], axis=0)

    def z_grad_finish(t, k):
        z_finish(grad_z.at[t], k)
        grad_full[t, own_chunk] = jnp.sum(grad_z[t], axis=0)

    grad_img[0, 0] = tn(uq[0], pke[0], P_GRAD) + tn(uq[1], pke[1], P_GRAD)
    grad_img[0, 1] = tn(uo[0], pve[0], P_GRAD) + tn(uo[1], pve[1], P_GRAD)
    pair_grad_start(0, 5)
    for b in two:
        ig_v[b] = dx[b] + tn(ds[b], kt[b], P_BACK)
    pair_grad_finish(0, 5)
    scatter_start(grad_pair.at[0], grad_rs.at[0], 6)
    finish(first_moments[0], 24)
    pass_on(0)

    loads[6].wait()
    filler = jnp.zeros((1, D), f32)
    query_cot = jnp.concatenate(
        [qc_v[i, b : b + 1] if i < 7 else filler for b in range(2) for i in range(8)], axis=0
    )
    plane_finish(c2_all, 4)
    c2 = jnp.sum(c2_all[...], axis=0)
    keep = ((row != 7) & (row != 15)).astype(f32)
    dpk_sum = c2[0:16] * keep
    dpv_sum = c2[16:32] * keep
    dg3 = jnp.concatenate([c2[7:8], c2[15:16]], axis=1)
    dc3 = jnp.concatenate([c2[23:24], c2[31:32]], axis=1)

    d_mlp = query_cot + nt(dpk_sum, cw[5], P_MIDB) + nt(dpv_sum, cw[6], P_MIDB)
    dg2, dc2 = col_sum(d_mlp * xhat2), col_sum(d_mlp)
    d2 = norm_back(d_mlp, xhat2, r2, row_of(vec, 2))
    d_hidden = nt(d2, mw[1], P_MIDB) * gelu_slope(hidden_in, cdf)
    wide_z[0, opt] = d_hidden
    narrow_z[opt] = d2

    @pl.when(core == 0)
    def _():
        z_start(wide_z.at[0], 7)

    z_start(narrow_z, 30)
    d_cross = d2 + nn(d_hidden, mw[0], P_MIDB)
    dg1, dc1 = col_sum(d_cross * xhat1), col_sum(d_cross)
    d1 = norm_back(d_cross, xhat1, r1, row_of(vec, 1))
    d_gathered = nn(d1, cw[3], P_MIDB)

    db_up = col_sum(d_hidden)
    vec_rows = [dg1, dg2, dg3, dc1, dc2, dc3, col_sum(d2), filler]
    vec_rows += [db_up[:, 256 * k : 256 * k + 256] for k in range(8)]
    small_z[opt] = jnp.concatenate(
        [
            d1,
            jnp.concatenate([gathered, pick(core, dpk_sum, dpv_sum)], axis=1),
            jnp.concatenate(vec_rows, axis=0),
        ],
        axis=0,
    )
    z_start(small_z, 31)
    for k in (1, 2):
        finish(first_moments[k], 24 + k)
        pass_on(k)
    scatter_finish(0, 6)
    z_start(grad_z.at[0], 9)

    pick_lane = (iota((64, 128), 1) == lax.div(iota((64, 128), 0), 8) * 16).astype(f32)

    def tiled(x, b):
        return jnp.concatenate([rows_of(x, b)] * 8, axis=0)

    dge = [expand(rows_of(d_gathered, b), mask64) for b in two]
    gt = [nt(dge[b], cw[2], P_SCOREB) for b in two]
    lse_col = [jnp.sum(tiled(lse, b) * pick_lane, axis=-1, keepdims=True) for b in two]
    p = [jnp.exp(s1_v[b] - lse_col[b]) for b in two]
    dot = [jnp.sum(dge[b] * tiled(gathered, b), axis=-1, keepdims=True) for b in two]
    ds = [p[b] * (nt(gt[b], image_v[b], P_SCOREB) - dot[b]) * CROSS_SCALE for b in two]
    uk = [nn(ds[b], image_v[b], P_SCOREB) for b in two]
    dq = [extract(nn(uk[b], cw[1], P_SCOREB), mask64) for b in two]
    c3_pair[core] = jnp.concatenate(dq, axis=0)
    pair_start(c3_pair, 10)
    uv = [nn(p[b], image_v[b], P_SCOREB) for b in two]
    grad_img[1, 0] = tn(uv[0], dge[0], P_GRAD) + tn(uv[1], dge[1], P_GRAD)
    grad_img[1, 1] = tn(uk[0], qe[0], P_GRAD) + tn(uk[1], qe[1], P_GRAD)
    pair_finish(c3_pair, 10)
    c3_all[chip] = c3_pair[0] + c3_pair[1]
    plane_start(c3_all, 11)
    pair_grad_start(1, 12)
    z_grad_finish(0, 9)
    gather_start(grad_full.at[0], 14)
    pair_grad_finish(1, 12)
    scatter_start(grad_pair.at[1], grad_rs.at[1], 13)
    for b in two:
        out_ig[b] = ig_v[b] + tn(ds[b], qt[b], P_SCOREB) + tn(p[b], gt[b], P_SCOREB)

    for src, dst, k in parts:
        pltpu.make_async_copy(src, dst, mom_sem.at[k]).wait()
    finish(last_moments[0], 27)
    z_finish(wide_z.at[core], 7)
    z_finish(early_z, 8)
    z_finish(narrow_z, 30)
    early = early_z[...]
    mlp_all = early[:, 0:16].reshape(64, D)
    beside = pick(core, early[:, 16:32], narrow_z[...]).reshape(64, D)
    m_new = MOMENTUM_DECAY * moment_m[...] + tn(wide_z[core].reshape(64, FF), beside, P_GRAD)
    moment_m[...] = m_new
    eye = (iota((D, D), 0) == iota((D, D), 1)).astype(f32)
    gram = tn(m_new, m_new, HIGHEST)
    scale_m = 1.0 / (jnp.sqrt(jnp.sum(gram * eye)) + SCALE_EPSILON)
    gram = gram * (scale_m * scale_m)

    def gram_sweep(gram, product, sweep):
        last = sweep + 1 == NS_ITERS
        prec = HIGHEST if sweep < 3 else HIGH
        poly = COEF_LINEAR * eye + COEF_CUBIC * gram + COEF_QUINTIC * nn(gram, gram, prec)
        half = None if last else nn(poly, gram, prec)
        product = poly if product is None else nn(product, poly, HIGHEST)
        return None if last else nn(half, poly, prec), product

    gram, product = gram_sweep(gram, None, 0)

    plane_finish(c3_all, 11)
    c3_z[opt] = jnp.sum(c3_all[...], axis=0)
    z_start(c3_z, 15)
    own_m = moment_m[mine_m]
    out_mm[core] = own_m
    remote(out_mm.at[core], out_mm.at[core], 17, sibling).start()
    scatter_finish(1, 13)
    z_start(grad_z.at[1], 16)

    z_finish(small_z, 31)
    small = small_z[...]
    d1_all = small[:, 0:16].reshape(64, D)
    pair_all = small[:, 16:32].reshape(64, D)
    vec_sum = jnp.sum(small[:, 32:48], axis=0)
    for k in (1, 2):
        finish(last_moments[k], 27 + k)
    fourth = tn(mlp_all, pair_all[:, 128:], P_GRAD)
    gather_finish(grad_full.at[0], 14)
    blocks = lax.div(iota((D, D), 0), 128) == lax.div(iota((D, D), 1), 128)

    def norm_scale(x):
        return 1.0 / (jnp.sqrt(jnp.sum(x * x)) + SCALE_EPSILON)

    def new_cross(j, grad):
        m = MOMENTUM_DECAY * moment_c[j] + grad
        moment_c[j] = m
        out_cm[cross_at[j]] = moment_c[j, mine_s]
        remote(out_cm.at[cross_at[j]], out_cm.at[cross_at[j]], 21, sibling).start()
        return m * norm_scale(m)

    def poly_of(x, paired):
        g = tn(x, x, P_SWEEP)
        if paired:
            g = jnp.where(blocks, g, 0.0)
        return COEF_CUBIC * g + COEF_QUINTIC * nn(g, g, P_SWEEP)

    def sweep_of(x, poly):
        return COEF_LINEAR * x + nn(x, poly, P_SWEEP)

    def own_rows(slot, x):
        last_x[slot] = x
        return last_x[slot, mine_s]

    rate = MATRIX_RATE * math.sqrt(D)
    decay = 1.0 - MATRIX_RATE * MATRIX_DECAY

    def put_cross(x, slots):
        for i, j in enumerate(slots):
            at = cross_at[j]
            out_cn[at] = decay * cw[at, mine_s] - rate * x[:, 128 * i : 128 * i + 128]
            remote(out_cn.at[at], out_cn.at[at], 23, sibling).start()

    x = jnp.concatenate([new_cross(0, grad_full[0]), new_cross(3, fourth)], axis=1)
    for sweep in range(1, NS_ITERS):
        gram, product = gram_sweep(gram, product, sweep)
        x = sweep_of(x, poly_of(x, True))
    put_cross(sweep_of(own_rows(0, x), poly_of(x, True)), (0, 3))
    out_mn[core] = decay * mw[core, mine_m] - (MATRIX_RATE * math.sqrt(FF)) * nn(own_m * scale_m, product, HIGHEST)
    remote(out_mn.at[core], out_mn.at[core], 18, sibling).start()

    z_finish(c3_z, 15)
    dq_all = c3_z[...].reshape(64, CROSS)
    z_grad_finish(1, 16)
    gather_start(grad_full.at[1], 19)
    d_after = d1_all + nt(dq_all, cw[0], P_FRONTB)
    dg0, dc0 = col_sum(d_after * xhat0), col_sum(d_after)
    d0 = norm_back(d_after, xhat0, r0, row_of(vec, 0))
    mask512 = head_mask(64, D)
    doe = expand(nt(d0, sw[3], P_FRONTB), mask512)
    da = nt(doe, v_s, P_FRONTB)
    ds = a_s * (da - jnp.sum(a_s * da, axis=-1, keepdims=True)) * SELF_SCALE
    dq_s = extract(nn(ds, k_s, P_FRONTB), mask512)
    dk_s = tn(ds, qe_s, P_FRONTB)
    dv_s = tn(a_s, doe, P_FRONTB)
    d_prompt = d0 + nt(dq_s, sw[0], P_FRONTB) + nt(dk_s, sw[1], P_FRONTB) + nt(dv_s, sw[2], P_FRONTB)
    label_all = pos[...].reshape(64, 128)[:, 2:3]
    d_label = [col_sum(jnp.where(label_all == float(k), d_prompt, 0.0)) for k in range(4)]

    norm_rows = [dg0] + [vec_sum[k : k + 1] for k in range(3)] + [dc0] + [vec_sum[k : k + 1] for k in range(3, 6)]
    vec_all = norm_rows + [vec_sum[8 + k : 9 + k] for k in range(8)] + [vec_sum[6:7]] + d_label
    for k, line in enumerate(vec_all):
        out_vec[2 * k : 2 * k + 1] = line[:, :128]
        out_vec[2 * k + 1 : 2 * k + 2] = line[:, 128:]

    first = tn(prompt_all, pick(core, dq_s, dv_s), P_GRAD)
    second = tn(pick(core, prompt_all, o_s), pick(core, dk_s, d0), P_GRAD)
    third = tn(pick(core, after_all, d1_all), pick(core, dq_all, pair_all[:, :128]), P_GRAD)
    gather_finish(grad_full.at[1], 19)
    self_m = [MOMENTUM_DECAY * moment_s[j] + g for j, g in enumerate((first, second))]
    for j in range(2):
        moment_s[j] = self_m[j]
        out_sm[2 * core + j] = moment_s[j, mine_s]
    own_s = pl.ds(2 * core, 2)
    remote(out_sm.at[own_s], out_sm.at[own_s], 20, sibling).start()
    xs = [m * norm_scale(m) for m in self_m]
    xs += [jnp.concatenate([new_cross(1, grad_full[1]), new_cross(2, third)], axis=1)]
    for sweep in range(NS_ITERS):
        polys = [poly_of(x, j == 2) for j, x in enumerate(xs)]
        if sweep + 1 == NS_ITERS:
            xs = [own_rows(1 + j, x) for j, x in enumerate(xs)]
        xs = [sweep_of(x, p) for x, p in zip(xs, polys)]
    for j in range(2):
        out_sn[2 * core + j] = decay * sw[2 * core + j, mine_s] - rate * xs[j]
    remote(out_sn.at[own_s], out_sn.at[own_s], 22, sibling).start()
    put_cross(xs[2], (1, 2))

    for buf, k in (
        (out_mm.at[0], 17),
        (out_mn.at[0], 18),
        (out_sm.at[pl.ds(0, 2)], 20),
        (out_cm.at[pl.ds(0, 4)], 21),
        (out_sn.at[pl.ds(0, 2)], 22),
        (out_cn.at[pl.ds(0, 4)], 23),
    ):
        finish(buf, k)


N_EXCHANGES = 32


def finish_kernel(*refs):
    sem = refs[-1]
    copies = [pltpu.make_async_copy(refs[i], refs[9 + i], sem.at[i]) for i in range(9)]
    for c in copies:
        c.start()
    for c in copies:
        c.wait()


def per_device(
    image,
    labels,
    coords,
    fourier,
    self_weights,
    cross_weights,
    mlp_weights,
    vectors,
    query_cot,
    key_cot,
    self_moment,
    cross_moment,
    mlp_moment,
    vec_first,
    vec_second,
):
    sds = lambda *s: jax.ShapeDtypeStruct(s, f32)
    out_shape = [
        sds(7, 2, 256),
        sds(2, 128, 256),
        sds(2, 128, 256),
        sds(4, 64, 256),
        sds(4, 64, 256),
        sds(8, 64, 128),
        sds(8, 64, 128),
        sds(2, 512, 256),
        sds(2, 512, 256),
        sds(42, 128),
    ]
    whole = pl.BlockSpec(memory_space=pl.ANY)
    inside = pl.BlockSpec(memory_space=pltpu.VMEM)
    scalars = pl.BlockSpec(memory_space=pltpu.SMEM)
    dma = pltpu.SemaphoreType.DMA
    v = lambda *s: pltpu.VMEM(s, f32)
    results = pl.pallas_call(
        kernel,
        out_shape=out_shape,
        in_specs=[scalars, scalars] + [whole] * 11,
        out_specs=[inside] * len(out_shape),
        scratch_shapes=[
            v(2, 128, 256),
            v(2, 128),
            v(4, 256, 256),
            v(8, 256, 128),
            v(2, 2048, 256),
            v(42, 128),
            v(7, 2, 256),
            v(2, 128, 256),
            v(2, 256, 256),
            v(4, 256, 128),
            v(2048, 256),
            v(4, 16, 128),
            v(2, 32, 128),
            v(16, 32, 128),
            v(2, 32, 128),
            v(16, 32, 128),
            v(2, 16, 128),
            v(16, 16, 128),
            v(4, 16, 128),
            v(2, 2, 256, 128),
            v(2, 256, 128),
            v(2, 16, 16, 128),
            v(2, 4, 16, 128),
            v(2, 256, 128),
            v(2, 4, 16, 2048),
            v(4, 32, 256),
            v(4, 16, 256),
            v(4, 48, 256),
            v(2, 64, 128),
            v(4, 256, 256),
            v(2, 128, 256),
            dma((8,)),
            dma((3,)),
            dma((N_EXCHANGES,)),
            dma((N_EXCHANGES,)),
        ],
        compiler_params=pltpu.CompilerParams(
            collective_id=0, has_side_effects=True, vmem_limit_bytes=60 * 2**20
        ),
    )(
        labels,
        coords.transpose(0, 2, 1),
        image,
        fourier,
        self_weights,
        cross_weights,
        mlp_weights,
        vectors.reshape(42, 128),
        query_cot.transpose(1, 0, 2),
        key_cot,
        self_moment,
        cross_moment,
        mlp_moment,
    )
    done = pl.pallas_call(
        finish_kernel,
        out_shape=out_shape[:9],
        in_specs=[inside] * 9,
        out_specs=[pl.BlockSpec(memory_space=pltpu.HBM)] * 9,
        scratch_shapes=[dma((9,))],
    )(*results[:9])
    share = vec_first.shape[0]
    at = lax.axis_index("opt") * share
    grad = lax.dynamic_slice_in_dim(results[9].reshape(-1), at, share, 0)
    local = lax.dynamic_slice_in_dim(vectors, at, share, 0)
    first = FIRST_DECAY * vec_first + (1.0 - FIRST_DECAY) * grad
    second = SECOND_DECAY * vec_second + (1.0 - SECOND_DECAY) * grad * grad
    direction = (
        first
        / (1.0 - FIRST_DECAY**STEP)
        / (jnp.sqrt(second / (1.0 - SECOND_DECAY**STEP)) + VECTOR_EPSILON)
    )
    return (
        done[0].transpose(1, 0, 2),
        *done[1:],
        first,
        second,
        local - VECTOR_RATE * direction,
    )


def solution(mesh):
    in_specs = (
        P("opt", "seq", None),
        P("opt", None),
        P("opt", None, None),
        P(),
        P(),
        P(),
        P(),
        P(),
        P("opt", None, None),
        P("opt", "seq", None),
        P(None, "opt", None),
        P(None, "opt", None),
        P(None, "opt", None),
        P("opt"),
        P("opt"),
    )
    out_specs = (
        P("opt", None, None),
        P("opt", "seq", None),
        P("opt", "seq", None),
        P(None, "opt", None),
        P(None, "opt", None),
        P(None, "opt", None),
        P(None, "opt", None),
        P(None, "opt", None),
        P(None, "opt", None),
        P("opt"),
        P("opt"),
        P("opt"),
    )
    return jax.shard_map(
        per_device, mesh=mesh, in_specs=in_specs, out_specs=out_specs, check_vma=False
    )
```

```python
import functools
import math

import jax
import jax.numpy as jnp
from jax import lax
from jax.experimental import pallas as pl
from jax.experimental.pallas import tpu as pltpu
from jax.sharding import PartitionSpec as P

D = 256
HEADS = 8
CROSS = 128
FF = 2048
IMG = 1024
NS_ITERS = 5
STEP = 10
NORM_EPSILON = 1e-05
COEF_LINEAR = 3.4445
COEF_CUBIC = -4.775
COEF_QUINTIC = 2.0315
MOMENTUM_DECAY = 0.95
MATRIX_RATE = 0.05
MATRIX_DECAY = 0.01
SCALE_EPSILON = 1e-07
VECTOR_RATE = 0.1
FIRST_DECAY = 0.9
SECOND_DECAY = 0.999
VECTOR_EPSILON = 1e-08

MESH = pl.DeviceIdType.MESH
f32 = jnp.float32
HIGH = lax.Precision.HIGH
HIGHEST = lax.Precision.HIGHEST
P_FRONT = HIGHEST
P_SCORE = HIGHEST
P_MID = HIGH
P_BACK = HIGH
P_MIDB = HIGH
P_SCOREB = HIGH
P_FRONTB = HIGH
P_GRAD = HIGH
P_SWEEP = HIGH
SELF_SCALE = 1.0 / math.sqrt(D // HEADS)
CROSS_SCALE = 1.0 / math.sqrt(CROSS // HEADS)
CROSS_OF = ((4, 7), (2, 1), (0, 3), (5, 6))


def mm(a, b, dims, prec):
    return lax.dot_general(a, b, (dims, ((), ())), precision=prec, preferred_element_type=f32)


def nn(a, b, prec):
    return mm(a, b, ((1,), (0,)), prec)


def nt(a, b, prec):
    return mm(a, b, ((1,), (1,)), prec)


def tn(a, b, prec):
    return mm(a, b, ((0,), (0,)), prec)


def iota(shape, dim):
    return lax.broadcasted_iota(jnp.int32, shape, dim)


def head_mask(rows, width):
    shape = (HEADS * rows, width)
    return (lax.div(iota(shape, 0), rows) == lax.div(iota(shape, 1), width // HEADS)).astype(f32)


def expand(x, mask):
    return jnp.concatenate([x] * HEADS, axis=0) * mask


def extract(u, mask):
    rows = u.shape[0] // HEADS
    return (u * mask).reshape(HEADS, rows, u.shape[1]).sum(axis=0)


def normed(x):
    center = x - jnp.mean(x, axis=-1, keepdims=True)
    r = lax.rsqrt(jnp.mean(center * center, axis=-1, keepdims=True) + NORM_EPSILON)
    return center * r, r


def norm_back(dy, xhat, r, gain):
    t = dy * gain
    return (t - jnp.mean(t, axis=-1, keepdims=True) - xhat * jnp.mean(t * xhat, axis=-1, keepdims=True)) * r


def col_sum(x):
    return jnp.sum(x, axis=0, keepdims=True)


def row_of(vec, k):
    return jnp.concatenate([vec[2 * k : 2 * k + 1], vec[2 * k + 1 : 2 * k + 2]], axis=1)


def embed(pos, fourier, vec):
    px = 2.0 * (pos[:, 0:1] + 0.5) / IMG - 1.0
    py = 2.0 * (pos[:, 1:2] + 0.5) / IMG - 1.0
    label = pos[:, 2:3]
    angles = 2.0 * math.pi * (px * fourier[0:1] + py * fourier[1:2])
    out = jnp.concatenate([jnp.sin(angles), jnp.cos(angles)], axis=1)
    for k in range(4):
        out = out + jnp.where(label == float(k), row_of(vec, 17 + k), 0.0)
    return out


def front(prompt, sw, vec):
    rows = prompt.shape[0]
    mask = head_mask(rows, D)
    q, k, v = (nn(prompt, sw[i], P_FRONT) for i in range(3))
    qe = expand(q, mask)
    shape = (HEADS * rows, rows)
    of_row = lax.div(lax.rem(iota(shape, 0), rows), 8)
    of_col = lax.div(iota(shape, 1), 8)
    valid = (of_row == of_col) & (lax.rem(iota(shape, 1), 8) != 7)
    s = jnp.where(valid, nt(qe, k, P_FRONT) * SELF_SCALE, -1e30)
    e = jnp.exp(s - jnp.max(s, axis=-1, keepdims=True))
    a = e / jnp.sum(e, axis=-1, keepdims=True)
    o = extract(nn(a, v, P_FRONT), mask)
    xhat, r = normed(prompt + nn(o, sw[3], P_FRONT))
    after = xhat * row_of(vec, 0) + row_of(vec, 4)
    return after, (qe, k, v, a, o, xhat, r)


def gelu_parts(x):
    cdf = 0.5 * (1.0 + lax.erf(x * (1.0 / math.sqrt(2.0))))
    return x * cdf, cdf


def gelu_slope(x, cdf):
    return cdf + x * jnp.exp(-0.5 * x * x) * (1.0 / math.sqrt(2.0 * math.pi))


def pick(core, a, b):
    return jnp.where(core == 0, a, b)


def kernel(
    labels,
    coords,
    image,
    fourier,
    sw_in,
    cw_in,
    mw_in,
    vec_in,
    qc,
    kc,
    sm_in,
    cm_in,
    mm_in,
    out_q,
    out_k,
    out_ig,
    out_sm,
    out_sn,
    out_cm,
    out_cn,
    out_mm,
    out_mn,
    out_vec,
    image_v,
    fourier_v,
    sw,
    cw,
    mw,
    vec_v,
    qc_v,
    kc_v,
    moment_s,
    moment_c,
    moment_m,
    pos,
    c1_pair,
    c1_all,
    c2_pair,
    c2_all,
    c3_pair,
    c3_all,
    c3_z,
    grad_img,
    grad_pair,
    grad_rs,
    grad_z,
    grad_full,
    wide_z,
    early_z,
    narrow_z,
    small_z,
    s1_v,
    last_x,
    ig_v,
    in_sem,
    mom_sem,
    send_sem,
    recv_sem,
):
    seq = lax.axis_index("seq")
    opt = lax.axis_index("opt")
    core = lax.rem(seq, 2)
    chip = lax.div(seq, 2)
    sibling = {"seq": seq + 1 - 2 * core}

    def across(i):
        return {"seq": 2 * lax.rem(chip + i, 16) + core}

    def along(i):
        return {"opt": lax.rem(opt + i, 4)}

    def remote(src, dst, k, to):
        return pltpu.make_async_remote_copy(src, dst, send_sem.at[k], recv_sem.at[k], to, MESH)

    def finish(ref, k):
        pltpu.make_async_copy(ref, ref, recv_sem.at[k]).wait()
        pltpu.make_async_copy(ref, ref, send_sem.at[k]).wait()

    def pair_start(buf, k):
        remote(buf.at[core], buf.at[core], k, sibling).start()

    def pair_finish(buf, k):
        finish(buf.at[0], k)

    def plane_start(buf, k):
        for i in range(1, 16):
            remote(buf.at[chip], buf.at[chip], k, across(i)).start()

    def plane_finish(buf, k):
        part = buf.at[pl.ds(0, 15)]
        finish(part, k)

    def z_start(buf, k):
        for i in range(1, 4):
            remote(buf.at[opt], buf.at[opt], k, along(i)).start()

    def z_finish(buf, k):
        part = buf.at[pl.ds(0, 3)]
        finish(part, k)

    def scatter_start(src, buf, k):
        for i in range(1, 16):
            to = lax.rem(chip + i, 16)
            remote(src.at[pl.ds(pl.multiple_of(to * 16, 16), 16)], buf.at[chip], k, across(i)).start()

    def gather_start(full, k):
        mine = full.at[pl.ds(pl.multiple_of(chip * 16, 16), 16)]
        for i in range(1, 16):
            remote(mine, mine, k, across(i)).start()

    def gather_finish(full, k):
        part = full.at[pl.ds(0, 240)]
        finish(part, k)

    barrier = pltpu.get_barrier_semaphore()
    peers = [sibling] + [across(i) for i in range(1, 16)] + [along(i) for i in range(1, 4)]
    for p in peers:
        pl.semaphore_signal(barrier, inc=1, device_id=p, device_id_type=MESH)
    loads = [
        pltpu.make_async_copy(src, dst, in_sem.at[i])
        for i, (src, dst) in enumerate(
            (
                (vec_in, vec_v),
                (fourier, fourier_v),
                (sw_in, sw),
                (cw_in, cw),
                (image, image_v),
                (mw_in, mw),
                (qc, qc_v),
                (kc, kc_v),
            )
        )
    ]
    for c in loads:
        c.start()

    lane = iota((16, 128), 1)
    row = iota((16, 128), 0)
    tile = jnp.zeros((16, 128), f32)
    for b in range(2):
        for i in range(7):
            here = row == 8 * b + i
            for c, value in enumerate((coords[b, 0, i], coords[b, 1, i], labels[b, i])):
                tile = jnp.where(here & (lane == c), value.astype(f32), tile)
    pos[opt] = tile

    for c in loads[:4]:
        c.wait()
    vec = vec_v[...]
    after_self, _ = front(embed(tile, fourier_v[...], vec), sw, vec)
    queries = nn(after_self, cw[0], P_FRONT)

    pl.semaphore_wait(barrier, len(peers))

    z_start(pos, 0)
    mine_m = pl.ds(pl.multiple_of(opt * 512, 512), 512)
    cross_at = [a + (b - a) * core for a, b in CROSS_OF]
    odd = lax.rem(chip, 2)
    tile_rows = pl.ds(pl.multiple_of(lax.div(chip, 2) * 8, 8), 8)
    tile_lanes = pl.ds(pl.multiple_of(odd * 128, 128), 128)
    own_s = pl.ds(2 * core, 2)
    fetched = [(mm_in.at[core], moment_m.at[mine_m], 0, (1, 3))]
    fetched += [(sm_in.at[own_s, tile_rows, tile_lanes], moment_s.at[:, opt, tile_rows, tile_lanes], 1, (1, 2, 3))]
    for t in range(2):
        at = cross_at[t] + (cross_at[2 + t] - cross_at[t]) * odd
        fetched += [(cm_in.at[at, tile_rows], moment_c.at[2 * odd + t, opt, tile_rows], 2, (1, 2, 3))]
    for src, dst, k, to in fetched[1:] + fetched[:1]:
        pltpu.make_async_copy(src, dst, mom_sem.at[k]).start()
        for i in to:
            remote(src, dst, 24 + k, along(i)).start()

    def pass_on():
        finish(moment_m.at[pl.ds(0, 1024)], 24)
        for i, half, to in ((3, 0, 1), (1, 1, 3)):
            start = lax.rem(opt + i, 4) * 512 + half * 256
            view = moment_m.at[pl.ds(pl.multiple_of(start, 256), 256)]
            remote(view, view, 27, along(to)).start()

    def spread_start(view, k):
        for src, dst, which, _ in fetched:
            if which == k:
                pltpu.make_async_copy(src, dst, mom_sem.at[k]).wait()
        finish(moment_m.at[pl.ds(0, 24)], 24 + k)
        for i in range(1, 16):
            remote(view, view, 27 + k, across(i)).start()

    def spread_finish(k):
        finish(moment_m.at[pl.ds(0, 480)], 27 + k)

    loads[4].wait()
    two = range(2)
    mask64 = head_mask(8, CROSS)

    def rows_of(x, b):
        return x[8 * b : 8 * b + 8]

    qe = [expand(rows_of(queries, b), mask64) for b in two]
    qt = [nt(qe[b], cw[1], P_SCORE) for b in two]
    s = [nt(qt[b], image_v[b], P_SCORE) * CROSS_SCALE for b in two]
    top = [jnp.max(s[b], axis=-1, keepdims=True) for b in two]
    e = [jnp.exp(s[b] - top[b]) for b in two]
    total = [jnp.sum(e[b], axis=-1, keepdims=True) for b in two]
    u = [nn(e[b], image_v[b], P_SCORE) / total[b] for b in two]
    o_parts = [extract(nn(u[b], cw[2], P_SCORE), mask64) for b in two]
    lse_parts = [extract(jnp.broadcast_to(top[b] + jnp.log(total[b]), (64, 128)), mask64) for b in two]
    for b in two:
        s1_v[b] = s[b]
    c1_pair[core] = jnp.concatenate(o_parts + lse_parts, axis=0)
    pair_start(c1_pair, 1)

    def joined(buf):
        o, lse = buf[:, 0:16], buf[:, 16:32]
        top = jnp.max(lse, axis=0)
        w = jnp.exp(lse - top[None])
        total = jnp.sum(w, axis=0)
        return jnp.sum(w * o, axis=0) / total, top + jnp.log(total)

    pair_finish(c1_pair, 1)
    c1_all[chip] = jnp.concatenate(joined(c1_pair), axis=0)
    plane_start(c1_all, 2)

    z_finish(pos, 0)
    prompt_all = embed(pos[...].reshape(64, 128), fourier_v[...], vec)
    after_all, (qe_s, k_s, v_s, a_s, o_s, xhat0, r0) = front(prompt_all, sw, vec)

    plane_finish(c1_all, 2)
    gathered, lse = joined(c1_all)
    spread_start(moment_s.at[:, :, tile_rows, tile_lanes], 1)

    xhat1, r1 = normed(after_self + nt(gathered, cw[3], P_MID))
    after_cross = xhat1 * row_of(vec, 1) + row_of(vec, 5)
    loads[5].wait()
    bias_up = jnp.concatenate([vec[16 + k : 17 + k] for k in range(16)], axis=1)
    hidden_in = nt(after_cross, mw[0], P_MID) + bias_up
    hidden, cdf = gelu_parts(hidden_in)
    xhat2, r2 = normed(after_cross + nn(hidden, mw[1], P_MID) + row_of(vec, 16))
    after_mlp = xhat2 * row_of(vec, 2) + row_of(vec, 6)
    for b in two:
        for i in range(7):
            out_q[i, b : b + 1] = after_mlp[8 * b + i : 8 * b + i + 1]
    prompt_keys = nn(after_mlp, cw[5], P_MID)
    prompt_values = nn(after_mlp, cw[6], P_MID)
    wide_z[1, opt] = hidden
    early_z[opt] = jnp.concatenate([after_mlp, after_cross], axis=0)
    @pl.when(core == 1)
    def _():
        z_start(wide_z.at[1], 7)

    z_start(early_z, 8)

    loads[7].wait()
    gain3, bias3 = row_of(vec, 3), row_of(vec, 7)
    real_row = lax.rem(iota((64, 128), 0), 8) != 7
    pke = [expand(rows_of(prompt_keys, b), mask64) for b in two]
    pve = [expand(rows_of(prompt_values, b), mask64) for b in two]
    kt = [nt(pke[b], cw[4], P_BACK) for b in two]
    vt = [nt(pve[b], cw[7], P_BACK) for b in two]
    s = [nt(kt[b], image_v[b], P_BACK) * CROSS_SCALE for b in two]
    s = [jnp.where(real_row, s[b], -1e30).reshape(8, 8, 128) for b in two]
    e = [jnp.exp(s[b] - jnp.max(s[b], axis=1, keepdims=True)) for b in two]
    a3 = [e[b] / jnp.sum(e[b], axis=1, keepdims=True) for b in two]
    a = [a3[b].reshape(64, 128) for b in two]
    n3 = [normed(image_v[b] + tn(a[b], vt[b], P_BACK)) for b in two]
    dx = [norm_back(kc_v[b], n3[b][0], n3[b][1], gain3) for b in two]
    da = [nt(vt[b], dx[b], P_BACK).reshape(8, 8, 128) for b in two]
    ds = [
        (a3[b] * (da[b] - jnp.sum(a3[b] * da[b], axis=1, keepdims=True)) * CROSS_SCALE).reshape(64, 128)
        for b in two
    ]
    uq = [nn(ds[b], image_v[b], P_BACK) for b in two]
    uo = [nn(a[b], dx[b], P_BACK) for b in two]
    dpk = [extract(nn(uq[b], cw[4], P_BACK), mask64) for b in two]
    dpv = [extract(nn(uo[b], cw[7], P_BACK), mask64) for b in two]
    dg3 = sum(col_sum(kc_v[b] * n3[b][0]) for b in two)
    dc3 = sum(col_sum(kc_v[b]) for b in two)
    fill = row == 7
    fill2 = row == 15

    def with_rows(x, first, second):
        return jnp.where(fill, first, jnp.where(fill2, second, x))

    c2_pair[core] = jnp.concatenate(
        [
            with_rows(jnp.concatenate(dpk, axis=0), dg3[:, :128], dg3[:, 128:]),
            with_rows(jnp.concatenate(dpv, axis=0), dc3[:, :128], dc3[:, 128:]),
        ],
        axis=0,
    )
    pair_start(c2_pair, 3)
    for b in two:
        out_k[b] = n3[b][0] * gain3 + bias3
    pair_finish(c2_pair, 3)
    c2_all[chip] = c2_pair[0] + c2_pair[1]
    plane_start(c2_all, 4)

    def pair_grad_start(t, k):
        remote(grad_img.at[t, 1 - core], grad_pair.at[t], k, sibling).start()

    def pair_grad_finish(t, k):
        finish(grad_pair.at[t], k)
        grad_pair[t] = grad_img[t, core] + grad_pair[t]

    own_chunk = pl.ds(pl.multiple_of(chip * 16, 16), 16)

    def scatter_finish(t, k):
        plane_finish(grad_rs.at[t], k)
        grad_rs[t, chip] = grad_pair[t, own_chunk]
        grad_z[t, opt] = jnp.sum(grad_rs[t], axis=0)

    def z_grad_finish(t, k):
        z_finish(grad_z.at[t], k)
        grad_full[t, own_chunk] = jnp.sum(grad_z[t], axis=0)

    grad_img[0, 0] = tn(uq[0], pke[0], P_GRAD) + tn(uq[1], pke[1], P_GRAD)
    grad_img[0, 1] = tn(uo[0], pve[0], P_GRAD) + tn(uo[1], pve[1], P_GRAD)
    pair_grad_start(0, 5)
    for b in two:
        ig_v[b] = dx[b] + tn(ds[b], kt[b], P_BACK)
    pair_grad_finish(0, 5)
    scatter_start(grad_pair.at[0], grad_rs.at[0], 6)
    pass_on()
    loads[6].wait()
    filler = jnp.zeros((1, D), f32)
    query_cot = jnp.concatenate(
        [qc_v[i, b : b + 1] if i < 7 else filler for b in range(2) for i in range(8)], axis=0
    )
    plane_finish(c2_all, 4)
    c2 = jnp.sum(c2_all[...], axis=0)
    keep = ((row != 7) & (row != 15)).astype(f32)
    dpk_sum = c2[0:16] * keep
    dpv_sum = c2[16:32] * keep
    dg3 = jnp.concatenate([c2[7:8], c2[15:16]], axis=1)
    dc3 = jnp.concatenate([c2[23:24], c2[31:32]], axis=1)
    spread_start(moment_c.at[pl.ds(2 * odd, 2), :, tile_rows], 2)

    d_mlp = query_cot + nt(dpk_sum, cw[5], P_MIDB) + nt(dpv_sum, cw[6], P_MIDB)
    dg2, dc2 = col_sum(d_mlp * xhat2), col_sum(d_mlp)
    d2 = norm_back(d_mlp, xhat2, r2, row_of(vec, 2))
    d_hidden = nt(d2, mw[1], P_MIDB) * gelu_slope(hidden_in, cdf)
    wide_z[0, opt] = d_hidden
    narrow_z[opt] = d2

    @pl.when(core == 0)
    def _():
        z_start(wide_z.at[0], 7)

    z_start(narrow_z, 30)
    d_cross = d2 + nn(d_hidden, mw[0], P_MIDB)
    dg1, dc1 = col_sum(d_cross * xhat1), col_sum(d_cross)
    d1 = norm_back(d_cross, xhat1, r1, row_of(vec, 1))
    d_gathered = nn(d1, cw[3], P_MIDB)

    db_up = col_sum(d_hidden)
    vec_rows = [dg1, dg2, dg3, dc1, dc2, dc3, col_sum(d2), filler]
    vec_rows += [db_up[:, 256 * k : 256 * k + 256] for k in range(8)]
    small_z[opt] = jnp.concatenate(
        [
            d1,
            jnp.concatenate([gathered, pick(core, dpk_sum, dpv_sum)], axis=1),
            jnp.concatenate(vec_rows, axis=0),
        ],
        axis=0,
    )
    z_start(small_z, 31)
    scatter_finish(0, 6)
    z_start(grad_z.at[0], 9)

    pick_lane = (iota((64, 128), 1) == lax.div(iota((64, 128), 0), 8) * 16).astype(f32)

    def tiled(x, b):
        return jnp.concatenate([rows_of(x, b)] * 8, axis=0)

    dge = [expand(rows_of(d_gathered, b), mask64) for b in two]
    gt = [nt(dge[b], cw[2], P_SCOREB) for b in two]
    lse_col = [jnp.sum(tiled(lse, b) * pick_lane, axis=-1, keepdims=True) for b in two]
    p = [jnp.exp(s1_v[b] - lse_col[b]) for b in two]
    dot = [jnp.sum(dge[b] * tiled(gathered, b), axis=-1, keepdims=True) for b in two]
    ds = [p[b] * (nt(gt[b], image_v[b], P_SCOREB) - dot[b]) * CROSS_SCALE for b in two]
    uk = [nn(ds[b], image_v[b], P_SCOREB) for b in two]
    dq = [extract(nn(uk[b], cw[1], P_SCOREB), mask64) for b in two]
    c3_pair[core] = jnp.concatenate(dq, axis=0)
    pair_start(c3_pair, 10)
    uv = [nn(p[b], image_v[b], P_SCOREB) for b in two]
    grad_img[1, 0] = tn(uv[0], dge[0], P_GRAD) + tn(uv[1], dge[1], P_GRAD)
    grad_img[1, 1] = tn(uk[0], qe[0], P_GRAD) + tn(uk[1], qe[1], P_GRAD)
    pair_finish(c3_pair, 10)
    c3_all[chip] = c3_pair[0] + c3_pair[1]
    plane_start(c3_all, 11)
    pair_grad_start(1, 12)
    z_grad_finish(0, 9)
    gather_start(grad_full.at[0], 14)
    pair_grad_finish(1, 12)
    scatter_start(grad_pair.at[1], grad_rs.at[1], 13)
    for b in two:
        out_ig[b] = ig_v[b] + tn(ds[b], qt[b], P_SCOREB) + tn(p[b], gt[b], P_SCOREB)

    pltpu.make_async_copy(*fetched[0][:2], mom_sem.at[0]).wait()
    finish(moment_m.at[pl.ds(0, 512)], 27)
    z_finish(wide_z.at[core], 7)
    z_finish(early_z, 8)
    z_finish(narrow_z, 30)
    early = early_z[...]
    mlp_all = early[:, 0:16].reshape(64, D)
    beside = pick(core, early[:, 16:32], narrow_z[...]).reshape(64, D)
    m_new = MOMENTUM_DECAY * moment_m[...] + tn(wide_z[core].reshape(64, FF), beside, P_GRAD)
    moment_m[...] = m_new
    eye = (iota((D, D), 0) == iota((D, D), 1)).astype(f32)
    gram = tn(m_new, m_new, HIGHEST)
    scale_m = 1.0 / (jnp.sqrt(jnp.sum(gram * eye)) + SCALE_EPSILON)
    gram = gram * (scale_m * scale_m)

    def gram_sweep(gram, product, sweep):
        last = sweep + 1 == NS_ITERS
        prec = HIGHEST if sweep < 3 else HIGH
        poly = COEF_LINEAR * eye + COEF_CUBIC * gram + COEF_QUINTIC * nn(gram, gram, prec)
        half = None if last else nn(poly, gram, prec)
        product = poly if product is None else nn(product, poly, HIGHEST)
        return None if last else nn(half, poly, prec), product

    gram, product = gram_sweep(gram, None, 0)

    plane_finish(c3_all, 11)
    c3_z[opt] = jnp.sum(c3_all[...], axis=0)
    z_start(c3_z, 15)
    own_m = moment_m[mine_m]
    out_mm[core] = own_m
    remote(out_mm.at[core], out_mm.at[core], 17, sibling).start()
    scatter_finish(1, 13)
    z_start(grad_z.at[1], 16)

    z_finish(small_z, 31)
    small = small_z[...]
    d1_all = small[:, 0:16].reshape(64, D)
    pair_all = small[:, 16:32].reshape(64, D)
    vec_sum = jnp.sum(small[:, 32:48], axis=0)
    spread_finish(2)
    fourth = tn(mlp_all, pair_all[:, 128:], P_GRAD)
    gather_finish(grad_full.at[0], 14)
    blocks = lax.div(iota((D, D), 0), 128) == lax.div(iota((D, D), 1), 128)

    def norm_scale(x):
        return 1.0 / (jnp.sqrt(jnp.sum(x * x)) + SCALE_EPSILON)

    def new_cross(j, grad):
        m = MOMENTUM_DECAY * moment_c[j].reshape(D, CROSS) + grad
        moment_c[j] = m.reshape(4, 64, CROSS)
        out_cm[cross_at[j]] = moment_c[j, opt]
        remote(out_cm.at[cross_at[j]], out_cm.at[cross_at[j]], 21, sibling).start()
        return m * norm_scale(m)

    def poly_of(x, paired):
        g = tn(x, x, P_SWEEP)
        if paired:
            g = jnp.where(blocks, g, 0.0)
        return COEF_CUBIC * g + COEF_QUINTIC * nn(g, g, P_SWEEP)

    def sweep_of(x, poly):
        return COEF_LINEAR * x + nn(x, poly, P_SWEEP)

    mine_s = pl.ds(pl.multiple_of(opt * 64, 64), 64)

    def own_rows(slot, x):
        last_x[slot] = x
        return last_x[slot, mine_s]

    rate = MATRIX_RATE * math.sqrt(D)
    decay = 1.0 - MATRIX_RATE * MATRIX_DECAY

    def put_cross(x, slots):
        for i, j in enumerate(slots):
            at = cross_at[j]
            out_cn[at] = decay * cw[at, mine_s] - rate * x[:, 128 * i : 128 * i + 128]
            remote(out_cn.at[at], out_cn.at[at], 23, sibling).start()

    x = jnp.concatenate([new_cross(0, grad_full[0]), new_cross(3, fourth)], axis=1)
    for sweep in range(1, NS_ITERS):
        gram, product = gram_sweep(gram, product, sweep)
        x = sweep_of(x, poly_of(x, True))
    put_cross(sweep_of(own_rows(0, x), poly_of(x, True)), (0, 3))
    out_mn[core] = decay * mw[core, mine_m] - (MATRIX_RATE * math.sqrt(FF)) * nn(own_m * scale_m, product, HIGHEST)
    remote(out_mn.at[core], out_mn.at[core], 18, sibling).start()

    z_finish(c3_z, 15)
    dq_all = c3_z[...].reshape(64, CROSS)
    z_grad_finish(1, 16)
    gather_start(grad_full.at[1], 19)
    d_after = d1_all + nt(dq_all, cw[0], P_FRONTB)
    dg0, dc0 = col_sum(d_after * xhat0), col_sum(d_after)
    d0 = norm_back(d_after, xhat0, r0, row_of(vec, 0))
    mask512 = head_mask(64, D)
    doe = expand(nt(d0, sw[3], P_FRONTB), mask512)
    da = nt(doe, v_s, P_FRONTB)
    ds = a_s * (da - jnp.sum(a_s * da, axis=-1, keepdims=True)) * SELF_SCALE
    dq_s = extract(nn(ds, k_s, P_FRONTB), mask512)
    dk_s = tn(ds, qe_s, P_FRONTB)
    dv_s = tn(a_s, doe, P_FRONTB)
    d_prompt = d0 + nt(dq_s, sw[0], P_FRONTB) + nt(dk_s, sw[1], P_FRONTB) + nt(dv_s, sw[2], P_FRONTB)
    label_all = pos[...].reshape(64, 128)[:, 2:3]
    d_label = [col_sum(jnp.where(label_all == float(k), d_prompt, 0.0)) for k in range(4)]

    norm_rows = [dg0] + [vec_sum[k : k + 1] for k in range(3)] + [dc0] + [vec_sum[k : k + 1] for k in range(3, 6)]
    vec_all = norm_rows + [vec_sum[8 + k : 9 + k] for k in range(8)] + [vec_sum[6:7]] + d_label
    for k, line in enumerate(vec_all):
        out_vec[2 * k : 2 * k + 1] = line[:, :128]
        out_vec[2 * k + 1 : 2 * k + 2] = line[:, 128:]

    first = tn(prompt_all, pick(core, dq_s, dv_s), P_GRAD)
    second = tn(pick(core, prompt_all, o_s), pick(core, dk_s, d0), P_GRAD)
    third = tn(pick(core, after_all, d1_all), pick(core, dq_all, pair_all[:, :128]), P_GRAD)
    gather_finish(grad_full.at[1], 19)
    spread_finish(1)
    self_m = [MOMENTUM_DECAY * moment_s[j].reshape(D, D) + g for j, g in enumerate((first, second))]
    for j in range(2):
        moment_s[j] = self_m[j].reshape(4, 64, D)
        out_sm[2 * core + j] = moment_s[j, opt]
    remote(out_sm.at[own_s], out_sm.at[own_s], 20, sibling).start()
    xs = [m * norm_scale(m) for m in self_m]
    xs += [jnp.concatenate([new_cross(1, grad_full[1]), new_cross(2, third)], axis=1)]
    for sweep in range(NS_ITERS):
        polys = [poly_of(x, j == 2) for j, x in enumerate(xs)]
        if sweep + 1 == NS_ITERS:
            xs = [own_rows(1 + j, x) for j, x in enumerate(xs)]
        xs = [sweep_of(x, p) for x, p in zip(xs, polys)]
    for j in range(2):
        out_sn[2 * core + j] = decay * sw[2 * core + j, mine_s] - rate * xs[j]
    remote(out_sn.at[own_s], out_sn.at[own_s], 22, sibling).start()
    put_cross(xs[2], (1, 2))

    for buf, k in (
        (out_mm.at[0], 17),
        (out_mn.at[0], 18),
        (out_sm.at[pl.ds(0, 2)], 20),
        (out_cm.at[pl.ds(0, 4)], 21),
        (out_sn.at[pl.ds(0, 2)], 22),
        (out_cn.at[pl.ds(0, 4)], 23),
    ):
        finish(buf, k)


N_EXCHANGES = 32


def finish_kernel(*refs):
    sem = refs[-1]
    copies = [pltpu.make_async_copy(refs[i], refs[9 + i], sem.at[i]) for i in range(9)]
    for c in copies:
        c.start()
    for c in copies:
        c.wait()


def per_device(
    image,
    labels,
    coords,
    fourier,
    self_weights,
    cross_weights,
    mlp_weights,
    vectors,
    query_cot,
    key_cot,
    self_moment,
    cross_moment,
    mlp_moment,
    vec_first,
    vec_second,
):
    sds = lambda *s: jax.ShapeDtypeStruct(s, f32)
    out_shape = [
        sds(7, 2, 256),
        sds(2, 128, 256),
        sds(2, 128, 256),
        sds(4, 64, 256),
        sds(4, 64, 256),
        sds(8, 64, 128),
        sds(8, 64, 128),
        sds(2, 512, 256),
        sds(2, 512, 256),
        sds(42, 128),
    ]
    whole = pl.BlockSpec(memory_space=pl.ANY)
    inside = pl.BlockSpec(memory_space=pltpu.VMEM)
    scalars = pl.BlockSpec(memory_space=pltpu.SMEM)
    dma = pltpu.SemaphoreType.DMA
    v = lambda *s: pltpu.VMEM(s, f32)
    results = pl.pallas_call(
        kernel,
        out_shape=out_shape,
        in_specs=[scalars, scalars] + [whole] * 11,
        out_specs=[inside] * len(out_shape),
        scratch_shapes=[
            v(2, 128, 256),
            v(2, 128),
            v(4, 256, 256),
            v(8, 256, 128),
            v(2, 2048, 256),
            v(42, 128),
            v(7, 2, 256),
            v(2, 128, 256),
            v(2, 4, 64, 256),
            v(4, 4, 64, 128),
            v(2048, 256),
            v(4, 16, 128),
            v(2, 32, 128),
            v(16, 32, 128),
            v(2, 32, 128),
            v(16, 32, 128),
            v(2, 16, 128),
            v(16, 16, 128),
            v(4, 16, 128),
            v(2, 2, 256, 128),
            v(2, 256, 128),
            v(2, 16, 16, 128),
            v(2, 4, 16, 128),
            v(2, 256, 128),
            v(2, 4, 16, 2048),
            v(4, 32, 256),
            v(4, 16, 256),
            v(4, 48, 256),
            v(2, 64, 128),
            v(4, 256, 256),
            v(2, 128, 256),
            dma((8,)),
            dma((3,)),
            dma((N_EXCHANGES,)),
            dma((N_EXCHANGES,)),
        ],
        compiler_params=pltpu.CompilerParams(
            collective_id=0, has_side_effects=True, vmem_limit_bytes=60 * 2**20
        ),
    )(
        labels,
        coords.transpose(0, 2, 1),
        image,
        fourier,
        self_weights,
        cross_weights,
        mlp_weights,
        vectors.reshape(42, 128),
        query_cot.transpose(1, 0, 2),
        key_cot,
        self_moment,
        cross_moment,
        mlp_moment,
    )
    done = pl.pallas_call(
        finish_kernel,
        out_shape=out_shape[:9],
        in_specs=[inside] * 9,
        out_specs=[pl.BlockSpec(memory_space=pltpu.HBM)] * 9,
        scratch_shapes=[dma((9,))],
    )(*results[:9])
    share = vec_first.shape[0]
    at = lax.axis_index("opt") * share
    grad = lax.dynamic_slice_in_dim(results[9].reshape(-1), at, share, 0)
    local = lax.dynamic_slice_in_dim(vectors, at, share, 0)
    first = FIRST_DECAY * vec_first + (1.0 - FIRST_DECAY) * grad
    second = SECOND_DECAY * vec_second + (1.0 - SECOND_DECAY) * grad * grad
    direction = (
        first
        / (1.0 - FIRST_DECAY**STEP)
        / (jnp.sqrt(second / (1.0 - SECOND_DECAY**STEP)) + VECTOR_EPSILON)
    )
    return (
        done[0].transpose(1, 0, 2),
        *done[1:],
        first,
        second,
        local - VECTOR_RATE * direction,
    )


def solution(mesh):
    in_specs = (
        P("opt", "seq", None),
        P("opt", None),
        P("opt", None, None),
        P(),
        P(),
        P(),
        P(),
        P(),
        P("opt", None, None),
        P("opt", "seq", None),
        P(None, "opt", None),
        P(None, "opt", None),
        P(None, "opt", None),
        P("opt"),
        P("opt"),
    )
    out_specs = (
        P("opt", None, None),
        P("opt", "seq", None),
        P("opt", "seq", None),
        P(None, "opt", None),
        P(None, "opt", None),
        P(None, "opt", None),
        P(None, "opt", None),
        P(None, "opt", None),
        P(None, "opt", None),
        P("opt"),
        P("opt"),
        P("opt"),
    )
    return jax.shard_map(
        per_device, mesh=mesh, in_specs=in_specs, out_specs=out_specs, check_vma=False
    )
```

```python
import functools
import math

import jax
import jax.numpy as jnp
from jax import lax
from jax.experimental import pallas as pl
from jax.experimental.pallas import tpu as pltpu
from jax.sharding import PartitionSpec as P

D = 256
HEADS = 8
CROSS = 128
FF = 2048
IMG = 1024
NS_ITERS = 5
STEP = 10
NORM_EPSILON = 1e-05
COEF_LINEAR = 3.4445
COEF_CUBIC = -4.775
COEF_QUINTIC = 2.0315
MOMENTUM_DECAY = 0.95
MATRIX_RATE = 0.05
MATRIX_DECAY = 0.01
SCALE_EPSILON = 1e-07
VECTOR_RATE = 0.1
FIRST_DECAY = 0.9
SECOND_DECAY = 0.999
VECTOR_EPSILON = 1e-08

MESH = pl.DeviceIdType.MESH
f32 = jnp.float32
HIGH = lax.Precision.HIGH
HIGHEST = lax.Precision.HIGHEST
P_FRONT = HIGHEST
P_SCORE = HIGHEST
P_MID = HIGH
P_BACK = HIGH
P_MIDB = HIGH
P_SCOREB = HIGH
P_FRONTB = HIGH
P_GRAD = HIGH
P_SWEEP = HIGH
SELF_SCALE = 1.0 / math.sqrt(D // HEADS)
CROSS_SCALE = 1.0 / math.sqrt(CROSS // HEADS)
CROSS_OF = ((4, 7), (2, 1), (0, 3), (5, 6))


def mm(a, b, dims, prec):
    return lax.dot_general(a, b, (dims, ((), ())), precision=prec, preferred_element_type=f32)


def nn(a, b, prec):
    return mm(a, b, ((1,), (0,)), prec)


def nt(a, b, prec):
    return mm(a, b, ((1,), (1,)), prec)


def tn(a, b, prec):
    return mm(a, b, ((0,), (0,)), prec)


def iota(shape, dim):
    return lax.broadcasted_iota(jnp.int32, shape, dim)


def head_mask(rows, width):
    shape = (HEADS * rows, width)
    return (lax.div(iota(shape, 0), rows) == lax.div(iota(shape, 1), width // HEADS)).astype(f32)


def expand(x, mask):
    return jnp.concatenate([x] * HEADS, axis=0) * mask


def extract(u, mask):
    rows = u.shape[0] // HEADS
    return (u * mask).reshape(HEADS, rows, u.shape[1]).sum(axis=0)


def normed(x):
    center = x - jnp.mean(x, axis=-1, keepdims=True)
    r = lax.rsqrt(jnp.mean(center * center, axis=-1, keepdims=True) + NORM_EPSILON)
    return center * r, r


def norm_back(dy, xhat, r, gain):
    t = dy * gain
    return (t - jnp.mean(t, axis=-1, keepdims=True) - xhat * jnp.mean(t * xhat, axis=-1, keepdims=True)) * r


def col_sum(x):
    return jnp.sum(x, axis=0, keepdims=True)


def row_of(vec, k):
    return jnp.concatenate([vec[2 * k : 2 * k + 1], vec[2 * k + 1 : 2 * k + 2]], axis=1)


def embed(pos, fourier, vec):
    px = 2.0 * (pos[:, 0:1] + 0.5) / IMG - 1.0
    py = 2.0 * (pos[:, 1:2] + 0.5) / IMG - 1.0
    label = pos[:, 2:3]
    angles = 2.0 * math.pi * (px * fourier[0:1] + py * fourier[1:2])
    out = jnp.concatenate([jnp.sin(angles), jnp.cos(angles)], axis=1)
    for k in range(4):
        out = out + jnp.where(label == float(k), row_of(vec, 17 + k), 0.0)
    return out


def front(prompt, sw, vec):
    rows = prompt.shape[0]
    mask = head_mask(rows, D)
    q, k, v = (nn(prompt, sw[i], P_FRONT) for i in range(3))
    qe = expand(q, mask)
    shape = (HEADS * rows, rows)
    of_row = lax.div(lax.rem(iota(shape, 0), rows), 8)
    of_col = lax.div(iota(shape, 1), 8)
    valid = (of_row == of_col) & (lax.rem(iota(shape, 1), 8) != 7)
    s = jnp.where(valid, nt(qe, k, P_FRONT) * SELF_SCALE, -1e30)
    e = jnp.exp(s - jnp.max(s, axis=-1, keepdims=True))
    a = e / jnp.sum(e, axis=-1, keepdims=True)
    o = extract(nn(a, v, P_FRONT), mask)
    xhat, r = normed(prompt + nn(o, sw[3], P_FRONT))
    after = xhat * row_of(vec, 0) + row_of(vec, 4)
    return after, (qe, k, v, a, o, xhat, r)


def gelu_parts(x):
    cdf = 0.5 * (1.0 + lax.erf(x * (1.0 / math.sqrt(2.0))))
    return x * cdf, cdf


def gelu_slope(x, cdf):
    return cdf + x * jnp.exp(-0.5 * x * x) * (1.0 / math.sqrt(2.0 * math.pi))


def pick(core, a, b):
    return jnp.where(core == 0, a, b)


def kernel(
    labels,
    coords,
    image,
    fourier,
    sw_in,
    cw_in,
    mw_in,
    vec_in,
    qc,
    kc,
    sm_in,
    cm_in,
    mm_in,
    out_q,
    out_k,
    out_ig,
    out_sm,
    out_sn,
    out_cm,
    out_cn,
    out_mm,
    out_mn,
    out_vec,
    out_own,
    image_v,
    fourier_v,
    sw,
    cw,
    mw,
    vec_v,
    qc_v,
    kc_v,
    moment_s,
    moment_c,
    moment_m,
    pos,
    c1_pair,
    c1_all,
    c2_pair,
    c2_all,
    c3_pair,
    c3_all,
    c3_z,
    grad_img,
    grad_pair,
    grad_rs,
    grad_z,
    grad_full,
    wide_z,
    early_z,
    narrow_z,
    small_z,
    s1_v,
    last_x,
    vec_rows_v,
    ig_v,
    in_sem,
    mom_sem,
    send_sem,
    recv_sem,
):
    seq = lax.axis_index("seq")
    opt = lax.axis_index("opt")
    core = lax.rem(seq, 2)
    chip = lax.div(seq, 2)
    sibling = {"seq": seq + 1 - 2 * core}

    def across(i):
        return {"seq": 2 * lax.rem(chip + i, 16) + core}

    def along(i):
        return {"opt": lax.rem(opt + i, 4)}

    def remote(src, dst, k, to):
        return pltpu.make_async_remote_copy(src, dst, send_sem.at[k], recv_sem.at[k], to, MESH)

    def finish(ref, k):
        pltpu.make_async_copy(ref, ref, recv_sem.at[k]).wait()
        pltpu.make_async_copy(ref, ref, send_sem.at[k]).wait()

    def pair_start(buf, k):
        remote(buf.at[core], buf.at[core], k, sibling).start()

    def pair_finish(buf, k):
        finish(buf.at[0], k)

    def plane_start(buf, k):
        for i in range(1, 16):
            remote(buf.at[chip], buf.at[chip], k, across(i)).start()

    def plane_finish(buf, k):
        part = buf.at[pl.ds(0, 15)]
        finish(part, k)

    def z_start(buf, k):
        for i in range(1, 4):
            remote(buf.at[opt], buf.at[opt], k, along(i)).start()

    def z_finish(buf, k):
        part = buf.at[pl.ds(0, 3)]
        finish(part, k)

    def scatter_start(src, buf, k):
        for i in range(1, 16):
            to = lax.rem(chip + i, 16)
            remote(src.at[pl.ds(pl.multiple_of(to * 16, 16), 16)], buf.at[chip], k, across(i)).start()

    def gather_start(full, k):
        mine = full.at[pl.ds(pl.multiple_of(chip * 16, 16), 16)]
        for i in range(1, 16):
            remote(mine, mine, k, across(i)).start()

    def gather_finish(full, k):
        part = full.at[pl.ds(0, 240)]
        finish(part, k)

    barrier = pltpu.get_barrier_semaphore()
    peers = [sibling] + [across(i) for i in range(1, 16)] + [along(i) for i in range(1, 4)]
    for p in peers:
        pl.semaphore_signal(barrier, inc=1, device_id=p, device_id_type=MESH)
    loads = [
        pltpu.make_async_copy(src, dst, in_sem.at[i])
        for i, (src, dst) in enumerate(
            (
                (vec_in, vec_v.at[pl.ds(0, 42)]),
                (fourier, fourier_v),
                (sw_in, sw),
                (cw_in, cw),
                (image, image_v),
                (mw_in, mw),
                (qc, qc_v),
                (kc, kc_v),
            )
        )
    ]
    for c in loads:
        c.start()

    lane = iota((16, 128), 1)
    row = iota((16, 128), 0)
    tile = jnp.zeros((16, 128), f32)
    for b in range(2):
        for i in range(7):
            here = row == 8 * b + i
            for c, value in enumerate((coords[b, 0, i], coords[b, 1, i], labels[b, i])):
                tile = jnp.where(here & (lane == c), value.astype(f32), tile)
    pos[opt] = tile

    for c in loads[:4]:
        c.wait()
    vec = vec_v[0:42]
    after_self, _ = front(embed(tile, fourier_v[...], vec), sw, vec)
    queries = nn(after_self, cw[0], P_FRONT)

    pl.semaphore_wait(barrier, len(peers))

    z_start(pos, 0)
    mine_m = pl.ds(pl.multiple_of(opt * 512, 512), 512)
    cross_at = [a + (b - a) * core for a, b in CROSS_OF]
    odd = lax.rem(chip, 2)
    tile_rows = pl.ds(pl.multiple_of(lax.div(chip, 2) * 8, 8), 8)
    tile_lanes = pl.ds(pl.multiple_of(odd * 128, 128), 128)
    own_s = pl.ds(2 * core, 2)
    fetched = [(mm_in.at[core], moment_m.at[mine_m], 0, (1, 3))]
    fetched += [(sm_in.at[own_s, tile_rows, tile_lanes], moment_s.at[:, opt, tile_rows, tile_lanes], 1, (1, 2, 3))]
    for t in range(2):
        at = cross_at[t] + (cross_at[2 + t] - cross_at[t]) * odd
        fetched += [(cm_in.at[at, tile_rows], moment_c.at[2 * odd + t, opt, tile_rows], 2, (1, 2, 3))]
    for src, dst, k, to in fetched[1:] + fetched[:1]:
        pltpu.make_async_copy(src, dst, mom_sem.at[k]).start()
        for i in to:
            remote(src, dst, 24 + k, along(i)).start()

    def pass_on():
        finish(moment_m.at[pl.ds(0, 1024)], 24)
        for i, half, to in ((3, 0, 1), (1, 1, 3)):
            start = lax.rem(opt + i, 4) * 512 + half * 256
            view = moment_m.at[pl.ds(pl.multiple_of(start, 256), 256)]
            remote(view, view, 27, along(to)).start()

    def spread_start(view, k):
        for src, dst, which, _ in fetched:
            if which == k:
                pltpu.make_async_copy(src, dst, mom_sem.at[k]).wait()
        finish(moment_m.at[pl.ds(0, 24)], 24 + k)
        for i in range(1, 16):
            remote(view, view, 27 + k, across(i)).start()

    def spread_finish(k):
        finish(moment_m.at[pl.ds(0, 480)], 27 + k)

    loads[4].wait()
    two = range(2)
    mask64 = head_mask(8, CROSS)

    def rows_of(x, b):
        return x[8 * b : 8 * b + 8]

    qe = [expand(rows_of(queries, b), mask64) for b in two]
    qt = [nt(qe[b], cw[1], P_SCORE) for b in two]
    s = [nt(qt[b], image_v[b], P_SCORE) * CROSS_SCALE for b in two]
    top = [jnp.max(s[b], axis=-1, keepdims=True) for b in two]
    e = [jnp.exp(s[b] - top[b]) for b in two]
    total = [jnp.sum(e[b], axis=-1, keepdims=True) for b in two]
    u = [nn(e[b], image_v[b], P_SCORE) / total[b] for b in two]
    o_parts = [extract(nn(u[b], cw[2], P_SCORE), mask64) for b in two]
    lse_parts = [extract(jnp.broadcast_to(top[b] + jnp.log(total[b]), (64, 128)), mask64) for b in two]
    for b in two:
        s1_v[b] = s[b]
    c1_pair[core] = jnp.concatenate(o_parts + lse_parts, axis=0)
    pair_start(c1_pair, 1)

    def joined(buf):
        o, lse = buf[:, 0:16], buf[:, 16:32]
        top = jnp.max(lse, axis=0)
        w = jnp.exp(lse - top[None])
        total = jnp.sum(w, axis=0)
        return jnp.sum(w * o, axis=0) / total, top + jnp.log(total)

    pair_finish(c1_pair, 1)
    c1_all[chip] = jnp.concatenate(joined(c1_pair), axis=0)
    plane_start(c1_all, 2)

    z_finish(pos, 0)
    prompt_all = embed(pos[...].reshape(64, 128), fourier_v[...], vec)
    after_all, (qe_s, k_s, v_s, a_s, o_s, xhat0, r0) = front(prompt_all, sw, vec)

    plane_finish(c1_all, 2)
    gathered, lse = joined(c1_all)
    spread_start(moment_s.at[:, :, tile_rows, tile_lanes], 1)

    xhat1, r1 = normed(after_self + nt(gathered, cw[3], P_MID))
    after_cross = xhat1 * row_of(vec, 1) + row_of(vec, 5)
    loads[5].wait()
    bias_up = jnp.concatenate([vec[16 + k : 17 + k] for k in range(16)], axis=1)
    hidden_in = nt(after_cross, mw[0], P_MID) + bias_up
    hidden, cdf = gelu_parts(hidden_in)
    xhat2, r2 = normed(after_cross + nn(hidden, mw[1], P_MID) + row_of(vec, 16))
    after_mlp = xhat2 * row_of(vec, 2) + row_of(vec, 6)
    for b in two:
        for i in range(7):
            out_q[i, b : b + 1] = after_mlp[8 * b + i : 8 * b + i + 1]
    prompt_keys = nn(after_mlp, cw[5], P_MID)
    prompt_values = nn(after_mlp, cw[6], P_MID)
    wide_z[1, opt] = hidden
    early_z[opt] = jnp.concatenate([after_mlp, after_cross], axis=0)
    @pl.when(core == 1)
    def _():
        z_start(wide_z.at[1], 7)

    z_start(early_z, 8)

    loads[7].wait()
    gain3, bias3 = row_of(vec, 3), row_of(vec, 7)
    real_row = lax.rem(iota((64, 128), 0), 8) != 7
    pke = [expand(rows_of(prompt_keys, b), mask64) for b in two]
    pve = [expand(rows_of(prompt_values, b), mask64) for b in two]
    kt = [nt(pke[b], cw[4], P_BACK) for b in two]
    vt = [nt(pve[b], cw[7], P_BACK) for b in two]
    s = [nt(kt[b], image_v[b], P_BACK) * CROSS_SCALE for b in two]
    s = [jnp.where(real_row, s[b], -1e30).reshape(8, 8, 128) for b in two]
    e = [jnp.exp(s[b] - jnp.max(s[b], axis=1, keepdims=True)) for b in two]
    a3 = [e[b] / jnp.sum(e[b], axis=1, keepdims=True) for b in two]
    a = [a3[b].reshape(64, 128) for b in two]
    n3 = [normed(image_v[b] + tn(a[b], vt[b], P_BACK)) for b in two]
    dx = [norm_back(kc_v[b], n3[b][0], n3[b][1], gain3) for b in two]
    da = [nt(vt[b], dx[b], P_BACK).reshape(8, 8, 128) for b in two]
    ds = [
        (a3[b] * (da[b] - jnp.sum(a3[b] * da[b], axis=1, keepdims=True)) * CROSS_SCALE).reshape(64, 128)
        for b in two
    ]
    uq = [nn(ds[b], image_v[b], P_BACK) for b in two]
    uo = [nn(a[b], dx[b], P_BACK) for b in two]
    dpk = [extract(nn(uq[b], cw[4], P_BACK), mask64) for b in two]
    dpv = [extract(nn(uo[b], cw[7], P_BACK), mask64) for b in two]
    dg3 = sum(col_sum(kc_v[b] * n3[b][0]) for b in two)
    dc3 = sum(col_sum(kc_v[b]) for b in two)
    fill = row == 7
    fill2 = row == 15

    def with_rows(x, first, second):
        return jnp.where(fill, first, jnp.where(fill2, second, x))

    c2_pair[core] = jnp.concatenate(
        [
            with_rows(jnp.concatenate(dpk, axis=0), dg3[:, :128], dg3[:, 128:]),
            with_rows(jnp.concatenate(dpv, axis=0), dc3[:, :128], dc3[:, 128:]),
        ],
        axis=0,
    )
    pair_start(c2_pair, 3)
    for b in two:
        out_k[b] = n3[b][0] * gain3 + bias3
    pair_finish(c2_pair, 3)
    c2_all[chip] = c2_pair[0] + c2_pair[1]
    plane_start(c2_all, 4)

    def pair_grad_start(t, k):
        remote(grad_img.at[t, 1 - core], grad_pair.at[t], k, sibling).start()

    def pair_grad_finish(t, k):
        finish(grad_pair.at[t], k)
        grad_pair[t] = grad_img[t, core] + grad_pair[t]

    own_chunk = pl.ds(pl.multiple_of(chip * 16, 16), 16)

    def scatter_finish(t, k):
        plane_finish(grad_rs.at[t], k)
        grad_rs[t, chip] = grad_pair[t, own_chunk]
        grad_z[t, opt] = jnp.sum(grad_rs[t], axis=0)

    def z_grad_finish(t, k):
        z_finish(grad_z.at[t], k)
        grad_full[t, own_chunk] = jnp.sum(grad_z[t], axis=0)

    grad_img[0, 0] = tn(uq[0], pke[0], P_GRAD) + tn(uq[1], pke[1], P_GRAD)
    grad_img[0, 1] = tn(uo[0], pve[0], P_GRAD) + tn(uo[1], pve[1], P_GRAD)
    pair_grad_start(0, 5)
    for b in two:
        ig_v[b] = dx[b] + tn(ds[b], kt[b], P_BACK)
    pair_grad_finish(0, 5)
    scatter_start(grad_pair.at[0], grad_rs.at[0], 6)
    pass_on()
    loads[6].wait()
    filler = jnp.zeros((1, D), f32)
    query_cot = jnp.concatenate(
        [qc_v[i, b : b + 1] if i < 7 else filler for b in range(2) for i in range(8)], axis=0
    )
    plane_finish(c2_all, 4)
    c2 = jnp.sum(c2_all[...], axis=0)
    keep = ((row != 7) & (row != 15)).astype(f32)
    dpk_sum = c2[0:16] * keep
    dpv_sum = c2[16:32] * keep
    dg3 = jnp.concatenate([c2[7:8], c2[15:16]], axis=1)
    dc3 = jnp.concatenate([c2[23:24], c2[31:32]], axis=1)
    spread_start(moment_c.at[pl.ds(2 * odd, 2), :, tile_rows], 2)

    d_mlp = query_cot + nt(dpk_sum, cw[5], P_MIDB) + nt(dpv_sum, cw[6], P_MIDB)
    dg2, dc2 = col_sum(d_mlp * xhat2), col_sum(d_mlp)
    d2 = norm_back(d_mlp, xhat2, r2, row_of(vec, 2))
    d_hidden = nt(d2, mw[1], P_MIDB) * gelu_slope(hidden_in, cdf)
    wide_z[0, opt] = d_hidden
    narrow_z[opt] = d2

    @pl.when(core == 0)
    def _():
        z_start(wide_z.at[0], 7)

    z_start(narrow_z, 30)
    d_cross = d2 + nn(d_hidden, mw[0], P_MIDB)
    dg1, dc1 = col_sum(d_cross * xhat1), col_sum(d_cross)
    d1 = norm_back(d_cross, xhat1, r1, row_of(vec, 1))
    d_gathered = nn(d1, cw[3], P_MIDB)

    db_up = col_sum(d_hidden)
    vec_rows = [dg1, dg2, dg3, dc1, dc2, dc3, col_sum(d2), filler]
    vec_rows += [db_up[:, 256 * k : 256 * k + 256] for k in range(8)]
    small_z[opt] = jnp.concatenate(
        [
            d1,
            jnp.concatenate([gathered, pick(core, dpk_sum, dpv_sum)], axis=1),
            jnp.concatenate(vec_rows, axis=0),
        ],
        axis=0,
    )
    z_start(small_z, 31)
    scatter_finish(0, 6)
    z_start(grad_z.at[0], 9)

    pick_lane = (iota((64, 128), 1) == lax.div(iota((64, 128), 0), 8) * 16).astype(f32)

    def tiled(x, b):
        return jnp.concatenate([rows_of(x, b)] * 8, axis=0)

    dge = [expand(rows_of(d_gathered, b), mask64) for b in two]
    gt = [nt(dge[b], cw[2], P_SCOREB) for b in two]
    lse_col = [jnp.sum(tiled(lse, b) * pick_lane, axis=-1, keepdims=True) for b in two]
    p = [jnp.exp(s1_v[b] - lse_col[b]) for b in two]
    dot = [jnp.sum(dge[b] * tiled(gathered, b), axis=-1, keepdims=True) for b in two]
    ds = [p[b] * (nt(gt[b], image_v[b], P_SCOREB) - dot[b]) * CROSS_SCALE for b in two]
    uk = [nn(ds[b], image_v[b], P_SCOREB) for b in two]
    dq = [extract(nn(uk[b], cw[1], P_SCOREB), mask64) for b in two]
    c3_pair[core] = jnp.concatenate(dq, axis=0)
    pair_start(c3_pair, 10)
    uv = [nn(p[b], image_v[b], P_SCOREB) for b in two]
    grad_img[1, 0] = tn(uv[0], dge[0], P_GRAD) + tn(uv[1], dge[1], P_GRAD)
    grad_img[1, 1] = tn(uk[0], qe[0], P_GRAD) + tn(uk[1], qe[1], P_GRAD)
    pair_finish(c3_pair, 10)
    c3_all[chip] = c3_pair[0] + c3_pair[1]
    plane_start(c3_all, 11)
    pair_grad_start(1, 12)
    z_grad_finish(0, 9)
    gather_start(grad_full.at[0], 14)
    pair_grad_finish(1, 12)
    scatter_start(grad_pair.at[1], grad_rs.at[1], 13)
    for b in two:
        out_ig[b] = ig_v[b] + tn(ds[b], qt[b], P_SCOREB) + tn(p[b], gt[b], P_SCOREB)

    pltpu.make_async_copy(*fetched[0][:2], mom_sem.at[0]).wait()
    finish(moment_m.at[pl.ds(0, 512)], 27)
    z_finish(wide_z.at[core], 7)
    z_finish(early_z, 8)
    z_finish(narrow_z, 30)
    early = early_z[...]
    mlp_all = early[:, 0:16].reshape(64, D)
    beside = pick(core, early[:, 16:32], narrow_z[...]).reshape(64, D)
    m_new = MOMENTUM_DECAY * moment_m[...] + tn(wide_z[core].reshape(64, FF), beside, P_GRAD)
    moment_m[...] = m_new
    eye = (iota((D, D), 0) == iota((D, D), 1)).astype(f32)
    gram = tn(m_new, m_new, HIGHEST)
    scale_m = 1.0 / (jnp.sqrt(jnp.sum(gram * eye)) + SCALE_EPSILON)
    gram = gram * (scale_m * scale_m)

    def gram_sweep(gram, product, sweep):
        last = sweep + 1 == NS_ITERS
        prec = HIGHEST if sweep < 3 else HIGH
        poly = COEF_LINEAR * eye + COEF_CUBIC * gram + COEF_QUINTIC * nn(gram, gram, prec)
        half = None if last else nn(poly, gram, prec)
        product = poly if product is None else nn(product, poly, HIGHEST)
        return None if last else nn(half, poly, prec), product

    gram, product = gram_sweep(gram, None, 0)

    plane_finish(c3_all, 11)
    c3_z[opt] = jnp.sum(c3_all[...], axis=0)
    z_start(c3_z, 15)
    own_m = moment_m[mine_m]
    out_mm[core] = own_m
    remote(out_mm.at[core], out_mm.at[core], 17, sibling).start()
    scatter_finish(1, 13)
    z_start(grad_z.at[1], 16)

    z_finish(small_z, 31)
    small = small_z[...]
    d1_all = small[:, 0:16].reshape(64, D)
    pair_all = small[:, 16:32].reshape(64, D)
    vec_sum = jnp.sum(small[:, 32:48], axis=0)
    spread_finish(2)
    fourth = tn(mlp_all, pair_all[:, 128:], P_GRAD)
    gather_finish(grad_full.at[0], 14)
    blocks = lax.div(iota((D, D), 0), 128) == lax.div(iota((D, D), 1), 128)

    def norm_scale(x):
        return 1.0 / (jnp.sqrt(jnp.sum(x * x)) + SCALE_EPSILON)

    def new_cross(j, grad):
        m = MOMENTUM_DECAY * moment_c[j].reshape(D, CROSS) + grad
        moment_c[j] = m.reshape(4, 64, CROSS)
        out_cm[cross_at[j]] = moment_c[j, opt]
        remote(out_cm.at[cross_at[j]], out_cm.at[cross_at[j]], 21, sibling).start()
        return m * norm_scale(m)

    def poly_of(x, paired):
        g = tn(x, x, P_SWEEP)
        if paired:
            g = jnp.where(blocks, g, 0.0)
        return COEF_CUBIC * g + COEF_QUINTIC * nn(g, g, P_SWEEP)

    def sweep_of(x, poly):
        return COEF_LINEAR * x + nn(x, poly, P_SWEEP)

    mine_s = pl.ds(pl.multiple_of(opt * 64, 64), 64)

    def own_rows(slot, x):
        last_x[slot] = x
        return last_x[slot, mine_s]

    rate = MATRIX_RATE * math.sqrt(D)
    decay = 1.0 - MATRIX_RATE * MATRIX_DECAY

    def put_cross(x, slots):
        for i, j in enumerate(slots):
            at = cross_at[j]
            out_cn[at] = decay * cw[at, mine_s] - rate * x[:, 128 * i : 128 * i + 128]
            remote(out_cn.at[at], out_cn.at[at], 23, sibling).start()

    x = jnp.concatenate([new_cross(0, grad_full[0]), new_cross(3, fourth)], axis=1)
    for sweep in range(1, NS_ITERS):
        gram, product = gram_sweep(gram, product, sweep)
        x = sweep_of(x, poly_of(x, True))
    put_cross(sweep_of(own_rows(0, x), poly_of(x, True)), (0, 3))
    out_mn[core] = decay * mw[core, mine_m] - (MATRIX_RATE * math.sqrt(FF)) * nn(own_m * scale_m, product, HIGHEST)
    remote(out_mn.at[core], out_mn.at[core], 18, sibling).start()

    z_finish(c3_z, 15)
    dq_all = c3_z[...].reshape(64, CROSS)
    z_grad_finish(1, 16)
    gather_start(grad_full.at[1], 19)
    d_after = d1_all + nt(dq_all, cw[0], P_FRONTB)
    dg0, dc0 = col_sum(d_after * xhat0), col_sum(d_after)
    d0 = norm_back(d_after, xhat0, r0, row_of(vec, 0))
    mask512 = head_mask(64, D)
    doe = expand(nt(d0, sw[3], P_FRONTB), mask512)
    da = nt(doe, v_s, P_FRONTB)
    ds = a_s * (da - jnp.sum(a_s * da, axis=-1, keepdims=True)) * SELF_SCALE
    dq_s = extract(nn(ds, k_s, P_FRONTB), mask512)
    dk_s = tn(ds, qe_s, P_FRONTB)
    dv_s = tn(a_s, doe, P_FRONTB)
    d_prompt = d0 + nt(dq_s, sw[0], P_FRONTB) + nt(dk_s, sw[1], P_FRONTB) + nt(dv_s, sw[2], P_FRONTB)
    label_all = pos[...].reshape(64, 128)[:, 2:3]
    d_label = [col_sum(jnp.where(label_all == float(k), d_prompt, 0.0)) for k in range(4)]

    norm_rows = [dg0] + [vec_sum[k : k + 1] for k in range(3)] + [dc0] + [vec_sum[k : k + 1] for k in range(3, 6)]
    vec_all = norm_rows + [vec_sum[8 + k : 9 + k] for k in range(8)] + [vec_sum[6:7]] + d_label
    for k, line in enumerate(vec_all):
        vec_rows_v[2 * k : 2 * k + 1] = line[:, :128]
        vec_rows_v[2 * k + 1 : 2 * k + 2] = line[:, 128:]
    vec_rows_v[42:48] = jnp.zeros((6, 128), f32)
    vec_v[42:48] = jnp.zeros((6, 128), f32)
    first_row = 10 * opt + lax.div(opt, 2)
    for src, dst in ((vec_rows_v, out_vec), (vec_v, out_own)):
        lines = src[pl.ds(first_row, 12)]
        turned = jnp.concatenate([lines[:, 64:], lines[:, :64]], axis=1)
        shifted = jnp.where(iota((11, 128), 1) < 64, turned[0:11], turned[1:12])
        dst[0:11] = jnp.where(lax.rem(opt, 2) == 0, lines[0:11], shifted)

    first = tn(prompt_all, pick(core, dq_s, dv_s), P_GRAD)
    second = tn(pick(core, prompt_all, o_s), pick(core, dk_s, d0), P_GRAD)
    third = tn(pick(core, after_all, d1_all), pick(core, dq_all, pair_all[:, :128]), P_GRAD)
    gather_finish(grad_full.at[1], 19)
    spread_finish(1)
    self_m = [MOMENTUM_DECAY * moment_s[j].reshape(D, D) + g for j, g in enumerate((first, second))]
    for j in range(2):
        moment_s[j] = self_m[j].reshape(4, 64, D)
        out_sm[2 * core + j] = moment_s[j, opt]
    remote(out_sm.at[own_s], out_sm.at[own_s], 20, sibling).start()
    xs = [m * norm_scale(m) for m in self_m]
    xs += [jnp.concatenate([new_cross(1, grad_full[1]), new_cross(2, third)], axis=1)]
    for sweep in range(NS_ITERS):
        polys = [poly_of(x, j == 2) for j, x in enumerate(xs)]
        if sweep + 1 == NS_ITERS:
            xs = [own_rows(1 + j, x) for j, x in enumerate(xs)]
        xs = [sweep_of(x, p) for x, p in zip(xs, polys)]
    for j in range(2):
        out_sn[2 * core + j] = decay * sw[2 * core + j, mine_s] - rate * xs[j]
    remote(out_sn.at[own_s], out_sn.at[own_s], 22, sibling).start()
    put_cross(xs[2], (1, 2))

    for buf, k in (
        (out_mm.at[0], 17),
        (out_mn.at[0], 18),
        (out_sm.at[pl.ds(0, 2)], 20),
        (out_cm.at[pl.ds(0, 4)], 21),
        (out_sn.at[pl.ds(0, 2)], 22),
        (out_cn.at[pl.ds(0, 4)], 23),
    ):
        finish(buf, k)


N_EXCHANGES = 32


def finish_kernel(*refs):
    sem = refs[-1]
    copies = [pltpu.make_async_copy(refs[i], refs[13 + i], sem.at[i]) for i in range(9)]
    for c in copies:
        c.start()
    grads, vectors, first_in, second_in = refs[9:13]
    first_out, second_out, vectors_out = refs[22:25]
    size = first_in.shape[0]
    for k, start in enumerate(range(0, size, 128)):
        width = min(128, size - start)
        at = pl.ds(start, width)
        grad = grads[k, pl.ds(0, width)]
        first = FIRST_DECAY * first_in[at] + (1.0 - FIRST_DECAY) * grad
        second = SECOND_DECAY * second_in[at] + (1.0 - SECOND_DECAY) * grad * grad
        direction = (
            first
            / (1.0 - FIRST_DECAY**STEP)
            / (jnp.sqrt(second / (1.0 - SECOND_DECAY**STEP)) + VECTOR_EPSILON)
        )
        first_out[at] = first
        second_out[at] = second
        vectors_out[at] = vectors[k, pl.ds(0, width)] - VECTOR_RATE * direction
    for c in copies:
        c.wait()


def per_device(
    image,
    labels,
    coords,
    fourier,
    self_weights,
    cross_weights,
    mlp_weights,
    vectors,
    query_cot,
    key_cot,
    self_moment,
    cross_moment,
    mlp_moment,
    vec_first,
    vec_second,
):
    sds = lambda *s: jax.ShapeDtypeStruct(s, f32)
    out_shape = [
        sds(7, 2, 256),
        sds(2, 128, 256),
        sds(2, 128, 256),
        sds(4, 64, 256),
        sds(4, 64, 256),
        sds(8, 64, 128),
        sds(8, 64, 128),
        sds(2, 512, 256),
        sds(2, 512, 256),
        sds(16, 128),
        sds(16, 128),
    ]
    whole = pl.BlockSpec(memory_space=pl.ANY)
    inside = pl.BlockSpec(memory_space=pltpu.VMEM)
    scalars = pl.BlockSpec(memory_space=pltpu.SMEM)
    dma = pltpu.SemaphoreType.DMA
    v = lambda *s: pltpu.VMEM(s, f32)
    results = pl.pallas_call(
        kernel,
        out_shape=out_shape,
        in_specs=[scalars, scalars] + [whole] * 11,
        out_specs=[inside] * len(out_shape),
        scratch_shapes=[
            v(2, 128, 256),
            v(2, 128),
            v(4, 256, 256),
            v(8, 256, 128),
            v(2, 2048, 256),
            v(48, 128),
            v(7, 2, 256),
            v(2, 128, 256),
            v(2, 4, 64, 256),
            v(4, 4, 64, 128),
            v(2048, 256),
            v(4, 16, 128),
            v(2, 32, 128),
            v(16, 32, 128),
            v(2, 32, 128),
            v(16, 32, 128),
            v(2, 16, 128),
            v(16, 16, 128),
            v(4, 16, 128),
            v(2, 2, 256, 128),
            v(2, 256, 128),
            v(2, 16, 16, 128),
            v(2, 4, 16, 128),
            v(2, 256, 128),
            v(2, 4, 16, 2048),
            v(4, 32, 256),
            v(4, 16, 256),
            v(4, 48, 256),
            v(2, 64, 128),
            v(4, 256, 256),
            v(48, 128),
            v(2, 128, 256),
            dma((8,)),
            dma((3,)),
            dma((N_EXCHANGES,)),
            dma((N_EXCHANGES,)),
        ],
        compiler_params=pltpu.CompilerParams(
            collective_id=0, has_side_effects=True, vmem_limit_bytes=60 * 2**20
        ),
    )(
        labels,
        coords.transpose(0, 2, 1),
        image,
        fourier,
        self_weights,
        cross_weights,
        mlp_weights,
        vectors.reshape(42, 128),
        query_cot.transpose(1, 0, 2),
        key_cot,
        self_moment,
        cross_moment,
        mlp_moment,
    )
    done = pl.pallas_call(
        finish_kernel,
        out_shape=out_shape[:9] + [sds(*vec_first.shape)] * 3,
        in_specs=[inside] * 13,
        out_specs=[pl.BlockSpec(memory_space=pltpu.HBM)] * 9 + [inside] * 3,
        scratch_shapes=[dma((9,))],
    )(*results, vec_first, vec_second)
    return (done[0].transpose(1, 0, 2), *done[1:])


def solution(mesh):
    in_specs = (
        P("opt", "seq", None),
        P("opt", None),
        P("opt", None, None),
        P(),
        P(),
        P(),
        P(),
        P(),
        P("opt", None, None),
        P("opt", "seq", None),
        P(None, "opt", None),
        P(None, "opt", None),
        P(None, "opt", None),
        P("opt"),
        P("opt"),
    )
    out_specs = (
        P("opt", None, None),
        P("opt", "seq", None),
        P("opt", "seq", None),
        P(None, "opt", None),
        P(None, "opt", None),
        P(None, "opt", None),
        P(None, "opt", None),
        P(None, "opt", None),
        P(None, "opt", None),
        P("opt"),
        P("opt"),
        P("opt"),
    )
    return jax.shard_map(
        per_device, mesh=mesh, in_specs=in_specs, out_specs=out_specs, check_vma=False
    )
```

```python
import functools
import math

import jax
import jax.numpy as jnp
from jax import lax
from jax.experimental import pallas as pl
from jax.experimental.pallas import tpu as pltpu
from jax.sharding import PartitionSpec as P

D = 256
HEADS = 8
CROSS = 128
FF = 2048
IMG = 1024
NS_ITERS = 5
STEP = 10
NORM_EPSILON = 1e-05
COEF_LINEAR = 3.4445
COEF_CUBIC = -4.775
COEF_QUINTIC = 2.0315
MOMENTUM_DECAY = 0.95
MATRIX_RATE = 0.05
MATRIX_DECAY = 0.01
SCALE_EPSILON = 1e-07
VECTOR_RATE = 0.1
FIRST_DECAY = 0.9
SECOND_DECAY = 0.999
VECTOR_EPSILON = 1e-08

MESH = pl.DeviceIdType.MESH


def hops(i):
    return min(i % 4, -i % 4) + min(i // 4, -(i // 4) % 4)


CHIPS = sorted(range(1, 16), key=hops, reverse=True)
LEVELS = (2, 1, 3)
f32 = jnp.float32
HIGH = lax.Precision.HIGH
HIGHEST = lax.Precision.HIGHEST
P_FRONT = HIGHEST
P_SCORE = HIGHEST
P_MID = HIGH
P_BACK = HIGH
P_MIDB = HIGH
P_SCOREB = HIGH
P_FRONTB = HIGH
P_GRAD = HIGH
P_SWEEP = HIGH
SELF_SCALE = 1.0 / math.sqrt(D // HEADS)
CROSS_SCALE = 1.0 / math.sqrt(CROSS // HEADS)
CROSS_OF = ((4, 7), (2, 1), (0, 3), (5, 6))


def mm(a, b, dims, prec):
    return lax.dot_general(a, b, (dims, ((), ())), precision=prec, preferred_element_type=f32)


def nn(a, b, prec):
    return mm(a, b, ((1,), (0,)), prec)


def nt(a, b, prec):
    return mm(a, b, ((1,), (1,)), prec)


def tn(a, b, prec):
    return mm(a, b, ((0,), (0,)), prec)


def iota(shape, dim):
    return lax.broadcasted_iota(jnp.int32, shape, dim)


def head_mask(rows, width):
    shape = (HEADS * rows, width)
    return (lax.div(iota(shape, 0), rows) == lax.div(iota(shape, 1), width // HEADS)).astype(f32)


def expand(x, mask):
    return jnp.concatenate([x] * HEADS, axis=0) * mask


def extract(u, mask):
    rows = u.shape[0] // HEADS
    return (u * mask).reshape(HEADS, rows, u.shape[1]).sum(axis=0)


def normed(x):
    center = x - jnp.mean(x, axis=-1, keepdims=True)
    r = lax.rsqrt(jnp.mean(center * center, axis=-1, keepdims=True) + NORM_EPSILON)
    return center * r, r


def norm_back(dy, xhat, r, gain):
    t = dy * gain
    return (t - jnp.mean(t, axis=-1, keepdims=True) - xhat * jnp.mean(t * xhat, axis=-1, keepdims=True)) * r


def col_sum(x):
    return jnp.sum(x, axis=0, keepdims=True)


def row_of(vec, k):
    return jnp.concatenate([vec[2 * k : 2 * k + 1], vec[2 * k + 1 : 2 * k + 2]], axis=1)


def embed(pos, fourier, vec):
    px = 2.0 * (pos[:, 0:1] + 0.5) / IMG - 1.0
    py = 2.0 * (pos[:, 1:2] + 0.5) / IMG - 1.0
    label = pos[:, 2:3]
    angles = 2.0 * math.pi * (px * fourier[0:1] + py * fourier[1:2])
    out = jnp.concatenate([jnp.sin(angles), jnp.cos(angles)], axis=1)
    for k in range(4):
        out = out + jnp.where(label == float(k), row_of(vec, 17 + k), 0.0)
    return out


def front(prompt, sw, vec):
    rows = prompt.shape[0]
    mask = head_mask(rows, D)
    q, k, v = (nn(prompt, sw[i], P_FRONT) for i in range(3))
    qe = expand(q, mask)
    shape = (HEADS * rows, rows)
    of_row = lax.div(lax.rem(iota(shape, 0), rows), 8)
    of_col = lax.div(iota(shape, 1), 8)
    valid = (of_row == of_col) & (lax.rem(iota(shape, 1), 8) != 7)
    s = jnp.where(valid, nt(qe, k, P_FRONT) * SELF_SCALE, -1e30)
    e = jnp.exp(s - jnp.max(s, axis=-1, keepdims=True))
    a = e / jnp.sum(e, axis=-1, keepdims=True)
    o = extract(nn(a, v, P_FRONT), mask)
    xhat, r = normed(prompt + nn(o, sw[3], P_FRONT))
    after = xhat * row_of(vec, 0) + row_of(vec, 4)
    return after, (qe, k, v, a, o, xhat, r)


def gelu_parts(x):
    cdf = 0.5 * (1.0 + lax.erf(x * (1.0 / math.sqrt(2.0))))
    return x * cdf, cdf


def gelu_slope(x, cdf):
    return cdf + x * jnp.exp(-0.5 * x * x) * (1.0 / math.sqrt(2.0 * math.pi))


def pick(core, a, b):
    return jnp.where(core == 0, a, b)


def kernel(
    labels,
    coords,
    image,
    fourier,
    sw_in,
    cw_in,
    mw_in,
    vec_in,
    qc,
    kc,
    sm_in,
    cm_in,
    mm_in,
    out_q,
    out_k,
    out_ig,
    out_sm,
    out_sn,
    out_cm,
    out_cn,
    out_mm,
    out_mn,
    out_vec,
    out_own,
    image_v,
    fourier_v,
    sw,
    cw,
    mw,
    vec_v,
    qc_v,
    kc_v,
    moment_s,
    moment_c,
    moment_m,
    pos,
    c1_pair,
    c1_all,
    c2_pair,
    c2_all,
    c3_pair,
    c3_all,
    c3_z,
    grad_img,
    grad_pair,
    grad_rs,
    grad_z,
    grad_full,
    wide_z,
    early_z,
    narrow_z,
    small_z,
    s1_v,
    last_x,
    vec_rows_v,
    ig_v,
    in_sem,
    mom_sem,
    send_sem,
    recv_sem,
):
    seq = lax.axis_index("seq")
    opt = lax.axis_index("opt")
    core = lax.rem(seq, 2)
    chip = lax.div(seq, 2)
    sibling = {"seq": seq + 1 - 2 * core}

    def across(i):
        return {"seq": 2 * lax.rem(chip + i, 16) + core}

    def along(i):
        return {"opt": lax.rem(opt + i, 4)}

    def remote(src, dst, k, to):
        return pltpu.make_async_remote_copy(src, dst, send_sem.at[k], recv_sem.at[k], to, MESH)

    def finish(ref, k):
        pltpu.make_async_copy(ref, ref, recv_sem.at[k]).wait()
        pltpu.make_async_copy(ref, ref, send_sem.at[k]).wait()

    def pair_start(buf, k):
        remote(buf.at[core], buf.at[core], k, sibling).start()

    def pair_finish(buf, k):
        finish(buf.at[0], k)

    def plane_start(buf, k):
        for i in CHIPS:
            remote(buf.at[chip], buf.at[chip], k, across(i)).start()

    def plane_finish(buf, k):
        part = buf.at[pl.ds(0, 15)]
        finish(part, k)

    def z_start(buf, k):
        for i in LEVELS:
            remote(buf.at[opt], buf.at[opt], k, along(i)).start()

    def z_finish(buf, k):
        part = buf.at[pl.ds(0, 3)]
        finish(part, k)

    def scatter_start(src, buf, k):
        for i in CHIPS:
            to = lax.rem(chip + i, 16)
            remote(src.at[pl.ds(pl.multiple_of(to * 16, 16), 16)], buf.at[chip], k, across(i)).start()

    def gather_start(full, k):
        mine = full.at[pl.ds(pl.multiple_of(chip * 16, 16), 16)]
        for i in CHIPS:
            remote(mine, mine, k, across(i)).start()

    def gather_finish(full, k):
        part = full.at[pl.ds(0, 240)]
        finish(part, k)

    barrier = pltpu.get_barrier_semaphore()
    peers = [sibling] + [across(i) for i in range(1, 16)] + [along(i) for i in range(1, 4)]
    for p in peers:
        pl.semaphore_signal(barrier, inc=1, device_id=p, device_id_type=MESH)
    loads = [
        pltpu.make_async_copy(src, dst, in_sem.at[i])
        for i, (src, dst) in enumerate(
            (
                (vec_in, vec_v.at[pl.ds(0, 42)]),
                (fourier, fourier_v),
                (sw_in, sw),
                (cw_in, cw),
                (image, image_v),
                (mw_in, mw),
                (qc, qc_v),
                (kc, kc_v),
            )
        )
    ]
    for c in loads:
        c.start()

    lane = iota((16, 128), 1)
    row = iota((16, 128), 0)
    tile = jnp.zeros((16, 128), f32)
    for b in range(2):
        for i in range(7):
            here = row == 8 * b + i
            for c, value in enumerate((coords[b, 0, i], coords[b, 1, i], labels[b, i])):
                tile = jnp.where(here & (lane == c), value.astype(f32), tile)
    pos[opt] = tile

    for c in loads[:4]:
        c.wait()
    vec = vec_v[0:42]
    after_self, _ = front(embed(tile, fourier_v[...], vec), sw, vec)
    queries = nn(after_self, cw[0], P_FRONT)

    pl.semaphore_wait(barrier, len(peers))

    z_start(pos, 0)
    mine_m = pl.ds(pl.multiple_of(opt * 512, 512), 512)
    cross_at = [a + (b - a) * core for a, b in CROSS_OF]
    odd = lax.rem(chip, 2)
    tile_rows = pl.ds(pl.multiple_of(lax.div(chip, 2) * 8, 8), 8)
    tile_lanes = pl.ds(pl.multiple_of(odd * 128, 128), 128)
    own_s = pl.ds(2 * core, 2)
    fetched = [(mm_in.at[core], moment_m.at[mine_m], 0, (1, 3))]
    fetched += [(sm_in.at[own_s, tile_rows, tile_lanes], moment_s.at[:, opt, tile_rows, tile_lanes], 1, (1, 2, 3))]
    for t in range(2):
        at = cross_at[t] + (cross_at[2 + t] - cross_at[t]) * odd
        fetched += [(cm_in.at[at, tile_rows], moment_c.at[2 * odd + t, opt, tile_rows], 2, (1, 2, 3))]
    for src, dst, k, to in fetched[1:] + fetched[:1]:
        pltpu.make_async_copy(src, dst, mom_sem.at[k]).start()
        for i in to:
            remote(src, dst, 24 + k, along(i)).start()

    def pass_on():
        finish(moment_m.at[pl.ds(0, 1024)], 24)
        for i, half, to in ((3, 0, 1), (1, 1, 3)):
            start = lax.rem(opt + i, 4) * 512 + half * 256
            view = moment_m.at[pl.ds(pl.multiple_of(start, 256), 256)]
            remote(view, view, 27, along(to)).start()

    def spread_start(view, k):
        for src, dst, which, _ in fetched:
            if which == k:
                pltpu.make_async_copy(src, dst, mom_sem.at[k]).wait()
        finish(moment_m.at[pl.ds(0, 24)], 24 + k)
        for i in CHIPS:
            remote(view, view, 27 + k, across(i)).start()

    def spread_finish(k):
        finish(moment_m.at[pl.ds(0, 480)], 27 + k)

    loads[4].wait()
    two = range(2)
    mask64 = head_mask(8, CROSS)

    def rows_of(x, b):
        return x[8 * b : 8 * b + 8]

    qe = [expand(rows_of(queries, b), mask64) for b in two]
    qt = [nt(qe[b], cw[1], P_SCORE) for b in two]
    s = [nt(qt[b], image_v[b], P_SCORE) * CROSS_SCALE for b in two]
    top = [jnp.max(s[b], axis=-1, keepdims=True) for b in two]
    e = [jnp.exp(s[b] - top[b]) for b in two]
    total = [jnp.sum(e[b], axis=-1, keepdims=True) for b in two]
    u = [nn(e[b], image_v[b], P_SCORE) / total[b] for b in two]
    o_parts = [extract(nn(u[b], cw[2], P_SCORE), mask64) for b in two]
    lse_parts = [extract(jnp.broadcast_to(top[b] + jnp.log(total[b]), (64, 128)), mask64) for b in two]
    for b in two:
        s1_v[b] = s[b]
    c1_pair[core] = jnp.concatenate(o_parts + lse_parts, axis=0)
    pair_start(c1_pair, 1)

    def joined(buf):
        o, lse = buf[:, 0:16], buf[:, 16:32]
        top = jnp.max(lse, axis=0)
        w = jnp.exp(lse - top[None])
        total = jnp.sum(w, axis=0)
        return jnp.sum(w * o, axis=0) / total, top + jnp.log(total)

    pair_finish(c1_pair, 1)
    c1_all[chip] = jnp.concatenate(joined(c1_pair), axis=0)
    plane_start(c1_all, 2)

    z_finish(pos, 0)
    prompt_all = embed(pos[...].reshape(64, 128), fourier_v[...], vec)
    after_all, (qe_s, k_s, v_s, a_s, o_s, xhat0, r0) = front(prompt_all, sw, vec)

    plane_finish(c1_all, 2)
    gathered, lse = joined(c1_all)
    spread_start(moment_s.at[:, :, tile_rows, tile_lanes], 1)

    xhat1, r1 = normed(after_self + nt(gathered, cw[3], P_MID))
    after_cross = xhat1 * row_of(vec, 1) + row_of(vec, 5)
    loads[5].wait()
    bias_up = jnp.concatenate([vec[16 + k : 17 + k] for k in range(16)], axis=1)
    hidden_in = nt(after_cross, mw[0], P_MID) + bias_up
    hidden, cdf = gelu_parts(hidden_in)
    xhat2, r2 = normed(after_cross + nn(hidden, mw[1], P_MID) + row_of(vec, 16))
    after_mlp = xhat2 * row_of(vec, 2) + row_of(vec, 6)
    for b in two:
        for i in range(7):
            out_q[i, b : b + 1] = after_mlp[8 * b + i : 8 * b + i + 1]
    prompt_keys = nn(after_mlp, cw[5], P_MID)
    prompt_values = nn(after_mlp, cw[6], P_MID)
    wide_z[1, opt] = hidden
    early_z[opt] = jnp.concatenate([after_mlp, after_cross], axis=0)
    @pl.when(core == 1)
    def _():
        z_start(wide_z.at[1], 7)

    z_start(early_z, 8)

    loads[7].wait()
    gain3, bias3 = row_of(vec, 3), row_of(vec, 7)
    real_row = lax.rem(iota((64, 128), 0), 8) != 7
    pke = [expand(rows_of(prompt_keys, b), mask64) for b in two]
    pve = [expand(rows_of(prompt_values, b), mask64) for b in two]
    kt = [nt(pke[b], cw[4], P_BACK) for b in two]
    vt = [nt(pve[b], cw[7], P_BACK) for b in two]
    s = [nt(kt[b], image_v[b], P_BACK) * CROSS_SCALE for b in two]
    s = [jnp.where(real_row, s[b], -1e30).reshape(8, 8, 128) for b in two]
    e = [jnp.exp(s[b] - jnp.max(s[b], axis=1, keepdims=True)) for b in two]
    a3 = [e[b] / jnp.sum(e[b], axis=1, keepdims=True) for b in two]
    a = [a3[b].reshape(64, 128) for b in two]
    n3 = [normed(image_v[b] + tn(a[b], vt[b], P_BACK)) for b in two]
    dx = [norm_back(kc_v[b], n3[b][0], n3[b][1], gain3) for b in two]
    da = [nt(vt[b], dx[b], P_BACK).reshape(8, 8, 128) for b in two]
    ds = [
        (a3[b] * (da[b] - jnp.sum(a3[b] * da[b], axis=1, keepdims=True)) * CROSS_SCALE).reshape(64, 128)
        for b in two
    ]
    uq = [nn(ds[b], image_v[b], P_BACK) for b in two]
    uo = [nn(a[b], dx[b], P_BACK) for b in two]
    dpk = [extract(nn(uq[b], cw[4], P_BACK), mask64) for b in two]
    dpv = [extract(nn(uo[b], cw[7], P_BACK), mask64) for b in two]
    dg3 = sum(col_sum(kc_v[b] * n3[b][0]) for b in two)
    dc3 = sum(col_sum(kc_v[b]) for b in two)
    fill = row == 7
    fill2 = row == 15

    def with_rows(x, first, second):
        return jnp.where(fill, first, jnp.where(fill2, second, x))

    c2_pair[core] = jnp.concatenate(
        [
            with_rows(jnp.concatenate(dpk, axis=0), dg3[:, :128], dg3[:, 128:]),
            with_rows(jnp.concatenate(dpv, axis=0), dc3[:, :128], dc3[:, 128:]),
        ],
        axis=0,
    )
    pair_start(c2_pair, 3)
    for b in two:
        out_k[b] = n3[b][0] * gain3 + bias3
    pair_finish(c2_pair, 3)
    c2_all[chip] = c2_pair[0] + c2_pair[1]
    plane_start(c2_all, 4)

    def pair_grad_start(t, k):
        remote(grad_img.at[t, 1 - core], grad_pair.at[t], k, sibling).start()

    def pair_grad_finish(t, k):
        finish(grad_pair.at[t], k)
        grad_pair[t] = grad_img[t, core] + grad_pair[t]

    own_chunk = pl.ds(pl.multiple_of(chip * 16, 16), 16)

    def scatter_finish(t, k):
        plane_finish(grad_rs.at[t], k)
        grad_rs[t, chip] = grad_pair[t, own_chunk]
        grad_z[t, opt] = jnp.sum(grad_rs[t], axis=0)

    def z_grad_finish(t, k):
        z_finish(grad_z.at[t], k)
        grad_full[t, own_chunk] = jnp.sum(grad_z[t], axis=0)

    grad_img[0, 0] = tn(uq[0], pke[0], P_GRAD) + tn(uq[1], pke[1], P_GRAD)
    grad_img[0, 1] = tn(uo[0], pve[0], P_GRAD) + tn(uo[1], pve[1], P_GRAD)
    pair_grad_start(0, 5)
    for b in two:
        ig_v[b] = dx[b] + tn(ds[b], kt[b], P_BACK)
    pair_grad_finish(0, 5)
    scatter_start(grad_pair.at[0], grad_rs.at[0], 6)
    pass_on()
    loads[6].wait()
    filler = jnp.zeros((1, D), f32)
    query_cot = jnp.concatenate(
        [qc_v[i, b : b + 1] if i < 7 else filler for b in range(2) for i in range(8)], axis=0
    )
    plane_finish(c2_all, 4)
    c2 = jnp.sum(c2_all[...], axis=0)
    keep = ((row != 7) & (row != 15)).astype(f32)
    dpk_sum = c2[0:16] * keep
    dpv_sum = c2[16:32] * keep
    dg3 = jnp.concatenate([c2[7:8], c2[15:16]], axis=1)
    dc3 = jnp.concatenate([c2[23:24], c2[31:32]], axis=1)
    spread_start(moment_c.at[pl.ds(2 * odd, 2), :, tile_rows], 2)

    d_mlp = query_cot + nt(dpk_sum, cw[5], P_MIDB) + nt(dpv_sum, cw[6], P_MIDB)
    dg2, dc2 = col_sum(d_mlp * xhat2), col_sum(d_mlp)
    d2 = norm_back(d_mlp, xhat2, r2, row_of(vec, 2))
    d_hidden = nt(d2, mw[1], P_MIDB) * gelu_slope(hidden_in, cdf)
    wide_z[0, opt] = d_hidden
    narrow_z[opt] = d2

    @pl.when(core == 0)
    def _():
        z_start(wide_z.at[0], 7)

    z_start(narrow_z, 30)
    d_cross = d2 + nn(d_hidden, mw[0], P_MIDB)
    dg1, dc1 = col_sum(d_cross * xhat1), col_sum(d_cross)
    d1 = norm_back(d_cross, xhat1, r1, row_of(vec, 1))
    d_gathered = nn(d1, cw[3], P_MIDB)

    db_up = col_sum(d_hidden)
    vec_rows = [dg1, dg2, dg3, dc1, dc2, dc3, col_sum(d2), filler]
    vec_rows += [db_up[:, 256 * k : 256 * k + 256] for k in range(8)]
    small_z[opt] = jnp.concatenate(
        [
            d1,
            jnp.concatenate([gathered, pick(core, dpk_sum, dpv_sum)], axis=1),
            jnp.concatenate(vec_rows, axis=0),
        ],
        axis=0,
    )
    z_start(small_z, 31)

    pick_lane = (iota((64, 128), 1) == lax.div(iota((64, 128), 0), 8) * 16).astype(f32)

    def tiled(x, b):
        return jnp.concatenate([rows_of(x, b)] * 8, axis=0)

    dge = [expand(rows_of(d_gathered, b), mask64) for b in two]
    gt = [nt(dge[b], cw[2], P_SCOREB) for b in two]
    lse_col = [jnp.sum(tiled(lse, b) * pick_lane, axis=-1, keepdims=True) for b in two]
    p = [jnp.exp(s1_v[b] - lse_col[b]) for b in two]
    dot = [jnp.sum(dge[b] * tiled(gathered, b), axis=-1, keepdims=True) for b in two]
    ds = [p[b] * (nt(gt[b], image_v[b], P_SCOREB) - dot[b]) * CROSS_SCALE for b in two]
    uk = [nn(ds[b], image_v[b], P_SCOREB) for b in two]
    dq = [extract(nn(uk[b], cw[1], P_SCOREB), mask64) for b in two]
    c3_pair[core] = jnp.concatenate(dq, axis=0)
    pair_start(c3_pair, 10)
    scatter_finish(0, 6)
    z_start(grad_z.at[0], 9)
    uv = [nn(p[b], image_v[b], P_SCOREB) for b in two]
    grad_img[1, 0] = tn(uv[0], dge[0], P_GRAD) + tn(uv[1], dge[1], P_GRAD)
    grad_img[1, 1] = tn(uk[0], qe[0], P_GRAD) + tn(uk[1], qe[1], P_GRAD)
    pair_finish(c3_pair, 10)
    c3_all[chip] = c3_pair[0] + c3_pair[1]
    plane_start(c3_all, 11)
    pair_grad_start(1, 12)
    z_grad_finish(0, 9)
    gather_start(grad_full.at[0], 14)
    pair_grad_finish(1, 12)
    scatter_start(grad_pair.at[1], grad_rs.at[1], 13)
    for b in two:
        out_ig[b] = ig_v[b] + tn(ds[b], qt[b], P_SCOREB) + tn(p[b], gt[b], P_SCOREB)

    pltpu.make_async_copy(*fetched[0][:2], mom_sem.at[0]).wait()
    finish(moment_m.at[pl.ds(0, 512)], 27)
    z_finish(wide_z.at[core], 7)
    z_finish(early_z, 8)
    z_finish(narrow_z, 30)
    early = early_z[...]
    mlp_all = early[:, 0:16].reshape(64, D)
    beside = pick(core, early[:, 16:32], narrow_z[...]).reshape(64, D)
    m_new = MOMENTUM_DECAY * moment_m[...] + tn(wide_z[core].reshape(64, FF), beside, P_GRAD)
    moment_m[...] = m_new
    eye = (iota((D, D), 0) == iota((D, D), 1)).astype(f32)
    gram = tn(m_new, m_new, HIGHEST)
    scale_m = 1.0 / (jnp.sqrt(jnp.sum(gram * eye)) + SCALE_EPSILON)
    gram = gram * (scale_m * scale_m)

    def gram_sweep(gram, product, sweep):
        last = sweep + 1 == NS_ITERS
        prec = HIGHEST if sweep < 3 else HIGH
        poly = COEF_LINEAR * eye + COEF_CUBIC * gram + COEF_QUINTIC * nn(gram, gram, prec)
        half = None if last else nn(poly, gram, prec)
        product = poly if product is None else nn(product, poly, HIGHEST)
        return None if last else nn(half, poly, prec), product

    gram, product = gram_sweep(gram, None, 0)

    plane_finish(c3_all, 11)
    c3_z[opt] = jnp.sum(c3_all[...], axis=0)
    z_start(c3_z, 15)
    own_m = moment_m[mine_m]
    out_mm[core] = own_m
    remote(out_mm.at[core], out_mm.at[core], 17, sibling).start()
    scatter_finish(1, 13)
    z_start(grad_z.at[1], 16)

    z_finish(small_z, 31)
    small = small_z[...]
    d1_all = small[:, 0:16].reshape(64, D)
    pair_all = small[:, 16:32].reshape(64, D)
    vec_sum = jnp.sum(small[:, 32:48], axis=0)
    spread_finish(2)
    fourth = tn(mlp_all, pair_all[:, 128:], P_GRAD)
    gather_finish(grad_full.at[0], 14)
    blocks = lax.div(iota((D, D), 0), 128) == lax.div(iota((D, D), 1), 128)

    def norm_scale(x):
        return 1.0 / (jnp.sqrt(jnp.sum(x * x)) + SCALE_EPSILON)

    def new_cross(j, grad):
        m = MOMENTUM_DECAY * moment_c[j].reshape(D, CROSS) + grad
        moment_c[j] = m.reshape(4, 64, CROSS)
        out_cm[cross_at[j]] = moment_c[j, opt]
        remote(out_cm.at[cross_at[j]], out_cm.at[cross_at[j]], 21, sibling).start()
        return m * norm_scale(m)

    def poly_of(x, paired):
        g = tn(x, x, P_SWEEP)
        if paired:
            g = jnp.where(blocks, g, 0.0)
        return COEF_CUBIC * g + COEF_QUINTIC * nn(g, g, P_SWEEP)

    def sweep_of(x, poly):
        return COEF_LINEAR * x + nn(x, poly, P_SWEEP)

    mine_s = pl.ds(pl.multiple_of(opt * 64, 64), 64)

    def own_rows(slot, x):
        last_x[slot] = x
        return last_x[slot, mine_s]

    rate = MATRIX_RATE * math.sqrt(D)
    decay = 1.0 - MATRIX_RATE * MATRIX_DECAY

    def put_cross(x, slots):
        for i, j in enumerate(slots):
            at = cross_at[j]
            out_cn[at] = decay * cw[at, mine_s] - rate * x[:, 128 * i : 128 * i + 128]
            remote(out_cn.at[at], out_cn.at[at], 23, sibling).start()

    x = jnp.concatenate([new_cross(0, grad_full[0]), new_cross(3, fourth)], axis=1)
    for sweep in range(1, NS_ITERS):
        gram, product = gram_sweep(gram, product, sweep)
        x = sweep_of(x, poly_of(x, True))
    put_cross(sweep_of(own_rows(0, x), poly_of(x, True)), (0, 3))
    out_mn[core] = decay * mw[core, mine_m] - (MATRIX_RATE * math.sqrt(FF)) * nn(own_m * scale_m, product, HIGHEST)
    remote(out_mn.at[core], out_mn.at[core], 18, sibling).start()

    z_finish(c3_z, 15)
    dq_all = c3_z[...].reshape(64, CROSS)
    z_grad_finish(1, 16)
    gather_start(grad_full.at[1], 19)
    d_after = d1_all + nt(dq_all, cw[0], P_FRONTB)
    dg0, dc0 = col_sum(d_after * xhat0), col_sum(d_after)
    d0 = norm_back(d_after, xhat0, r0, row_of(vec, 0))
    mask512 = head_mask(64, D)
    doe = expand(nt(d0, sw[3], P_FRONTB), mask512)
    da = nt(doe, v_s, P_FRONTB)
    ds = a_s * (da - jnp.sum(a_s * da, axis=-1, keepdims=True)) * SELF_SCALE
    dq_s = extract(nn(ds, k_s, P_FRONTB), mask512)
    dk_s = tn(ds, qe_s, P_FRONTB)
    dv_s = tn(a_s, doe, P_FRONTB)
    d_prompt = d0 + nt(dq_s, sw[0], P_FRONTB) + nt(dk_s, sw[1], P_FRONTB) + nt(dv_s, sw[2], P_FRONTB)
    label_all = pos[...].reshape(64, 128)[:, 2:3]
    d_label = [col_sum(jnp.where(label_all == float(k), d_prompt, 0.0)) for k in range(4)]

    norm_rows = [dg0] + [vec_sum[k : k + 1] for k in range(3)] + [dc0] + [vec_sum[k : k + 1] for k in range(3, 6)]
    vec_all = norm_rows + [vec_sum[8 + k : 9 + k] for k in range(8)] + [vec_sum[6:7]] + d_label
    for k, line in enumerate(vec_all):
        vec_rows_v[2 * k : 2 * k + 1] = line[:, :128]
        vec_rows_v[2 * k + 1 : 2 * k + 2] = line[:, 128:]
    vec_rows_v[42:48] = jnp.zeros((6, 128), f32)
    vec_v[42:48] = jnp.zeros((6, 128), f32)
    first_row = 10 * opt + lax.div(opt, 2)
    for src, dst in ((vec_rows_v, out_vec), (vec_v, out_own)):
        lines = src[pl.ds(first_row, 12)]
        turned = jnp.concatenate([lines[:, 64:], lines[:, :64]], axis=1)
        shifted = jnp.where(iota((11, 128), 1) < 64, turned[0:11], turned[1:12])
        dst[0:11] = jnp.where(lax.rem(opt, 2) == 0, lines[0:11], shifted)

    first = tn(prompt_all, pick(core, dq_s, dv_s), P_GRAD)
    second = tn(pick(core, prompt_all, o_s), pick(core, dk_s, d0), P_GRAD)
    third = tn(pick(core, after_all, d1_all), pick(core, dq_all, pair_all[:, :128]), P_GRAD)
    gather_finish(grad_full.at[1], 19)
    spread_finish(1)
    self_m = [MOMENTUM_DECAY * moment_s[j].reshape(D, D) + g for j, g in enumerate((first, second))]
    for j in range(2):
        moment_s[j] = self_m[j].reshape(4, 64, D)
        out_sm[2 * core + j] = moment_s[j, opt]
    remote(out_sm.at[own_s], out_sm.at[own_s], 20, sibling).start()
    xs = [m * norm_scale(m) for m in self_m]
    xs += [jnp.concatenate([new_cross(1, grad_full[1]), new_cross(2, third)], axis=1)]
    for sweep in range(NS_ITERS):
        polys = [poly_of(x, j == 2) for j, x in enumerate(xs)]
        if sweep + 1 == NS_ITERS:
            xs = [own_rows(1 + j, x) for j, x in enumerate(xs)]
        xs = [sweep_of(x, p) for x, p in zip(xs, polys)]
    for j in range(2):
        out_sn[2 * core + j] = decay * sw[2 * core + j, mine_s] - rate * xs[j]
    remote(out_sn.at[own_s], out_sn.at[own_s], 22, sibling).start()
    put_cross(xs[2], (1, 2))

    for buf, k in (
        (out_mm.at[0], 17),
        (out_mn.at[0], 18),
        (out_sm.at[pl.ds(0, 2)], 20),
        (out_cm.at[pl.ds(0, 4)], 21),
        (out_sn.at[pl.ds(0, 2)], 22),
        (out_cn.at[pl.ds(0, 4)], 23),
    ):
        finish(buf, k)


N_EXCHANGES = 32


def finish_kernel(*refs):
    sem = refs[-1]
    copies = [pltpu.make_async_copy(refs[i], refs[13 + i], sem.at[i]) for i in range(9)]
    for c in copies:
        c.start()
    grads, vectors, first_in, second_in = refs[9:13]
    first_out, second_out, vectors_out = refs[22:25]
    size = first_in.shape[0]
    for k, start in enumerate(range(0, size, 128)):
        width = min(128, size - start)
        at = pl.ds(start, width)
        grad = grads[k, pl.ds(0, width)]
        first = FIRST_DECAY * first_in[at] + (1.0 - FIRST_DECAY) * grad
        second = SECOND_DECAY * second_in[at] + (1.0 - SECOND_DECAY) * grad * grad
        direction = (
            first
            / (1.0 - FIRST_DECAY**STEP)
            / (jnp.sqrt(second / (1.0 - SECOND_DECAY**STEP)) + VECTOR_EPSILON)
        )
        first_out[at] = first
        second_out[at] = second
        vectors_out[at] = vectors[k, pl.ds(0, width)] - VECTOR_RATE * direction
    for c in copies:
        c.wait()


def per_device(
    image,
    labels,
    coords,
    fourier,
    self_weights,
    cross_weights,
    mlp_weights,
    vectors,
    query_cot,
    key_cot,
    self_moment,
    cross_moment,
    mlp_moment,
    vec_first,
    vec_second,
):
    sds = lambda *s: jax.ShapeDtypeStruct(s, f32)
    out_shape = [
        sds(7, 2, 256),
        sds(2, 128, 256),
        sds(2, 128, 256),
        sds(4, 64, 256),
        sds(4, 64, 256),
        sds(8, 64, 128),
        sds(8, 64, 128),
        sds(2, 512, 256),
        sds(2, 512, 256),
        sds(16, 128),
        sds(16, 128),
    ]
    whole = pl.BlockSpec(memory_space=pl.ANY)
    inside = pl.BlockSpec(memory_space=pltpu.VMEM)
    scalars = pl.BlockSpec(memory_space=pltpu.SMEM)
    dma = pltpu.SemaphoreType.DMA
    v = lambda *s: pltpu.VMEM(s, f32)
    results = pl.pallas_call(
        kernel,
        out_shape=out_shape,
        in_specs=[scalars, scalars] + [whole] * 11,
        out_specs=[inside] * len(out_shape),
        scratch_shapes=[
            v(2, 128, 256),
            v(2, 128),
            v(4, 256, 256),
            v(8, 256, 128),
            v(2, 2048, 256),
            v(48, 128),
            v(7, 2, 256),
            v(2, 128, 256),
            v(2, 4, 64, 256),
            v(4, 4, 64, 128),
            v(2048, 256),
            v(4, 16, 128),
            v(2, 32, 128),
            v(16, 32, 128),
            v(2, 32, 128),
            v(16, 32, 128),
            v(2, 16, 128),
            v(16, 16, 128),
            v(4, 16, 128),
            v(2, 2, 256, 128),
            v(2, 256, 128),
            v(2, 16, 16, 128),
            v(2, 4, 16, 128),
            v(2, 256, 128),
            v(2, 4, 16, 2048),
            v(4, 32, 256),
            v(4, 16, 256),
            v(4, 48, 256),
            v(2, 64, 128),
            v(4, 256, 256),
            v(48, 128),
            v(2, 128, 256),
            dma((8,)),
            dma((3,)),
            dma((N_EXCHANGES,)),
            dma((N_EXCHANGES,)),
        ],
        compiler_params=pltpu.CompilerParams(
            collective_id=0, has_side_effects=True, vmem_limit_bytes=60 * 2**20
        ),
    )(
        labels,
        coords.transpose(0, 2, 1),
        image,
        fourier,
        self_weights,
        cross_weights,
        mlp_weights,
        vectors.reshape(42, 128),
        query_cot.transpose(1, 0, 2),
        key_cot,
        self_moment,
        cross_moment,
        mlp_moment,
    )
    done = pl.pallas_call(
        finish_kernel,
        out_shape=out_shape[:9] + [sds(*vec_first.shape)] * 3,
        in_specs=[inside] * 13,
        out_specs=[pl.BlockSpec(memory_space=pltpu.HBM)] * 9 + [inside] * 3,
        scratch_shapes=[dma((9,))],
    )(*results, vec_first, vec_second)
    return (done[0].transpose(1, 0, 2), *done[1:])


def solution(mesh):
    in_specs = (
        P("opt", "seq", None),
        P("opt", None),
        P("opt", None, None),
        P(),
        P(),
        P(),
        P(),
        P(),
        P("opt", None, None),
        P("opt", "seq", None),
        P(None, "opt", None),
        P(None, "opt", None),
        P(None, "opt", None),
        P("opt"),
        P("opt"),
    )
    out_specs = (
        P("opt", None, None),
        P("opt", "seq", None),
        P("opt", "seq", None),
        P(None, "opt", None),
        P(None, "opt", None),
        P(None, "opt", None),
        P(None, "opt", None),
        P(None, "opt", None),
        P(None, "opt", None),
        P("opt"),
        P("opt"),
        P("opt"),
    )
    return jax.shard_map(
        per_device, mesh=mesh, in_specs=in_specs, out_specs=out_specs, check_vma=False
    )
```
